1024 devices in a mesh: dp: 16 (over z_lo, core), expert: 64 (over z_hi, y, x).
Axes of the slice: x: 4, y: 4, z: 32 (z_hi: 4, z_lo: 8; z = z_hi * 8 + z_lo), core: 2. Of those that a mesh axis runs over, the one named last changes fastest.
Arguments:
- latent: bfloat16 [131072, 1024], P(('dp', 'expert')), may hold values from -6 to 6
- expert_ids: int32 [131072, 8], P(('dp', 'expert')), may hold values from 0 to 255, all different within a row
- gate_probs: float32 [131072, 8], P(('dp', 'expert')), may hold values from 0.05 to 1
- cotangent: bfloat16 [131072, 1024], P(('dp', 'expert')), may hold values from -6 to 6
- w_gate_up: bfloat16 [64, 1024, 1024], P('expert'), may hold values from -0.1875 to 0.1875
- w_down: bfloat16 [64, 1024, 512], P('expert'), may hold values from -0.25 to 0.25
Outputs:
- mixed: bfloat16 [131072, 1024], P(('dp', 'expert'))
- latent_gradient: bfloat16 [131072, 1024], P(('dp', 'expert'))
- gate_grad: float32 [131072, 8], P(('dp', 'expert'))
- gate_up_grad: bfloat16 [64, 1024, 1024], P('expert', 'dp')
- down_grad: bfloat16 [64, 1024, 512], P('expert', 'dp')
The draws below stay inside these ranges and needn't reach their ends.
All inputs are finite; a program needn't handle non-finite values.
Results may differ from the reference program's by a relative error of at most 0.023.
Values may be sent and summed in bfloat16 or wider, within the bound.
No kernel may reach another device: no remote copies, remote signals or barrier semaphores. Data moves between devices by JAX's collectives and lax.ppermute only.
A program may use at most 32 MiB of HBM per device.

```python
import math
import jax
import jax.numpy as jnp
from jax import lax

LAT = 1024
FFW = 512
TOP = 8
EXP_DEV = 4
CAP = 2
TOK_DEV = 128
FLIGHT = 64
EXPERTS = 256
TOKENS = 131072
N_DP = 16
N_EXPERT = 64


def shard_levels(key, dims, pieces, smallest, high):
    gain = 1.0
    for dim, parts in pieces:
        steps = jax.random.uniform(jax.random.fold_in(jax.random.fold_in(key, 6), dim), (parts,), jnp.float32, smallest / len(pieces), high / len(pieces))
        gain = gain * jnp.repeat(jnp.exp(steps), dims[dim] // parts).reshape((-1,) + (1,) * (len(dims) - 1 - dim))
    return gain


def different_ones(stream_key, rows, number_of, top, lift):
    ranking = jax.random.permutation(jax.random.fold_in(stream_key, 1), number_of)
    favour = ranking
    for power in range(3):
        favour = favour * favour // number_of
    favour = favour * lift // number_of
    lots = jax.random.randint(jax.random.fold_in(stream_key, 2), (rows, number_of), 0, 4096) + favour
    fixed_rows = jax.random.permutation(jax.random.fold_in(stream_key, 3), rows)[jnp.arange(number_of) % rows]
    lots = jnp.where(jnp.arange(rows)[:, None] == fixed_rows[None, :], 1 << 14, lots)
    score = lots * number_of + jnp.arange(number_of)
    return lax.top_k(score.astype(jnp.int32), top)[1].astype(jnp.int32)


def bell_draw(own_key, extent, width, limit, cuts=(), held_as=jnp.bfloat16):
    array = width * jax.random.normal(own_key, extent, jnp.float32)
    if cuts:
        array = array * shard_levels(own_key, extent, cuts, -0.22, 0.18)
    return jnp.clip(array, -limit, limit).astype(held_as)


def setup_inputs(seed: int = 0) -> dict:
    splits = jax.random.split(jax.random.key(seed), 7)
    latent = bell_draw(splits[0], (TOKENS, LAT), 1.0, 6.0, ((0, 1024),))
    expert_ids = different_ones(splits[1], TOKENS, EXPERTS, TOP, 0)
    gate_probs = jnp.clip(jnp.exp(math.log(1.0) - 2.9957323 * jax.random.uniform(splits[2], (TOKENS, TOP), jnp.float32) ** shard_levels(splits[2], (TOKENS, TOP), ((0, 1024),), -0.2, 0.2)), 0.05, 1.0)
    cotangent = bell_draw(splits[3], (TOKENS, LAT), 1.0, 6.0, ((0, 1024),))
    w_gate_up = bell_draw(splits[4], (FLIGHT, LAT, 2 * FFW), LAT ** -0.5, 0.1875, ((0, 64),))
    w_down = bell_draw(splits[5], (FLIGHT, LAT, FFW), FFW ** -0.5, 0.25, ((0, 64),))
    return dict(latent=latent, expert_ids=expert_ids, gate_probs=gate_probs, cotangent=cotangent, w_gate_up=w_gate_up, w_down=w_down)


def expert_step(incoming_rows, slot_cotangent, weight_in, output_weight):
    ffw_width = output_weight.shape[1]
    hidden = jnp.dot(incoming_rows, weight_in, preferred_element_type=jnp.float32)
    gate_part = hidden[:, :ffw_width]
    up_part = hidden[:, ffw_width:]
    silu_product = (jax.nn.silu(gate_part) * up_part).astype(jnp.bfloat16)
    expert_out = jnp.dot(silu_product, output_weight.T, preferred_element_type=jnp.float32).astype(jnp.bfloat16)
    grad_act = jnp.dot(slot_cotangent, output_weight, preferred_element_type=jnp.float32)
    sigmoid_gate = jax.nn.sigmoid(gate_part)
    grad_gate = grad_act * up_part * sigmoid_gate * (1.0 + gate_part * (1.0 - sigmoid_gate))
    grad_up = grad_act * gate_part * sigmoid_gate
    hidden_gradient = jnp.concatenate([grad_gate, grad_up], axis=1).astype(jnp.bfloat16)
    grad_rows = jnp.dot(hidden_gradient, weight_in.T, preferred_element_type=jnp.float32).astype(jnp.bfloat16)
    return expert_out, silu_product, hidden_gradient, grad_rows


def reference(latent, expert_ids, gate_probs, cotangent, w_gate_up, w_down):
    blocks = N_DP * N_EXPERT
    slot_count = FLIGHT * CAP
    ids_blocks = expert_ids.reshape(blocks, TOK_DEV, TOP)
    expert_axis = jnp.arange(EXPERTS, dtype=jnp.int32)
    one_hot = jnp.sum((ids_blocks[:, :, :, None] == expert_axis).astype(jnp.int32), axis=2)
    earlier = jnp.cumsum(one_hot, axis=1) - one_hot
    position = jnp.take_along_axis(earlier, ids_blocks, axis=2)
    kept = (ids_blocks % EXP_DEV == 0) & (position < CAP)
    target = jnp.where(kept, (ids_blocks // EXP_DEV) * CAP + position, slot_count).astype(jnp.int32)
    block_index = jnp.broadcast_to(jnp.arange(blocks, dtype=jnp.int32)[:, None, None], target.shape)
    slot_global = jnp.arange(TOKENS * TOP, dtype=jnp.int32).reshape(blocks, TOK_DEV, TOP)
    table = jnp.full((blocks, slot_count + 1), -1, jnp.int32)
    table = table.at[block_index, target].set(slot_global)
    table = table[:, :slot_count].reshape(N_DP, N_EXPERT, FLIGHT, CAP)
    gate_flat = gate_probs.reshape(-1)

    def one_expert(carry, column):
        mixed_sum, grad_sum, gate_sum = carry
        index_rows = lax.dynamic_index_in_dim(table, column, 2, keepdims=False).reshape(N_DP, N_EXPERT * CAP)
        valid = index_rows >= 0
        slot_index = jnp.where(valid, index_rows, 0)
        token_index = slot_index // TOP
        incoming_rows = jnp.where(valid[:, :, None], latent[token_index], jnp.zeros((), jnp.bfloat16))
        gate_rows = jnp.where(valid, gate_flat[slot_index], jnp.float32(0.0))
        slot_cotangent = (gate_rows[:, :, None] * cotangent[token_index].astype(jnp.float32)).astype(jnp.bfloat16)
        weight_in = w_gate_up[column]
        output_weight = w_down[column]
        expert_out, silu_product, hidden_gradient, grad_rows = expert_step(incoming_rows.reshape(-1, LAT), slot_cotangent.reshape(-1, LAT), weight_in, output_weight)
        expert_out = expert_out.reshape(N_DP, N_EXPERT * CAP, LAT)
        silu_product = silu_product.reshape(N_DP, N_EXPERT * CAP, FFW)
        hidden_gradient = hidden_gradient.reshape(N_DP, N_EXPERT * CAP, 2 * FFW)
        grad_rows = grad_rows.reshape(N_DP, N_EXPERT * CAP, LAT)
        up_projection_terms = jnp.einsum("sqx,squ->sxu", incoming_rows.astype(jnp.float32), hidden_gradient.astype(jnp.float32)).astype(jnp.bfloat16)
        down_projection_terms = jnp.einsum("sqx,squ->sxu", slot_cotangent.astype(jnp.float32), silu_product.astype(jnp.float32)).astype(jnp.bfloat16)
        up_grad = jnp.sum(up_projection_terms.astype(jnp.float32), axis=0).astype(jnp.bfloat16)
        down_part = jnp.sum(down_projection_terms.astype(jnp.float32), axis=0).astype(jnp.bfloat16)
        token_target = jnp.where(valid, token_index, TOKENS).reshape(-1)
        slot_target = jnp.where(valid, slot_index, TOKENS * TOP).reshape(-1)
        out_flat = expert_out.reshape(-1, LAT).astype(jnp.float32)
        mixed_sum = mixed_sum.at[token_target].add(gate_rows.reshape(-1)[:, None] * out_flat, mode="drop")
        grad_sum = grad_sum.at[token_target].add(grad_rows.reshape(-1, LAT).astype(jnp.float32), mode="drop")
        inner = jnp.sum(cotangent[token_index].astype(jnp.float32).reshape(-1, LAT) * out_flat, axis=1)
        gate_sum = gate_sum.at[slot_target].add(inner, mode="drop")
        return (mixed_sum, grad_sum, gate_sum), (up_grad, down_part)

    start = (jnp.zeros((TOKENS, LAT), jnp.float32), jnp.zeros((TOKENS, LAT), jnp.float32), jnp.zeros((TOKENS * TOP,), jnp.float32))
    (mixed_sum, grad_sum, gate_sum), (gate_up_grad, down_grad) = lax.scan(one_expert, start, jnp.arange(FLIGHT, dtype=jnp.int32))
    mixed = mixed_sum.astype(jnp.bfloat16)
    latent_gradient = grad_sum.astype(jnp.bfloat16)
    gate_grad = gate_sum.reshape(TOKENS, TOP)
    return mixed, latent_gradient, gate_grad, gate_up_grad, down_grad
```

```python
import jax
import jax.numpy as jnp
from jax import lax
from jax.sharding import PartitionSpec as P

EXP_DEV = 4
CAP = 2
F32 = jnp.float32
BF16 = jnp.bfloat16


def mm(a, b, ca, cb):
    return lax.dot_general(a, b, (((ca,), (cb,)), ((), ())), preferred_element_type=F32)


def halves(value):
    high = value.astype(BF16)
    return high, (value - high.astype(F32)).astype(BF16)


def route(expert_ids, gate_probs, columns):
    tokens = expert_ids.shape[0]
    rows = columns * 2 * CAP
    ids = expert_ids.T
    probs = gate_probs.T
    row = lax.broadcasted_iota(jnp.int32, (rows, tokens), 0)
    expert = row // (2 * CAP) * EXP_DEV
    named = jnp.zeros((rows, tokens), F32)
    gate = jnp.zeros((rows, tokens), F32)
    for slot in range(ids.shape[0]):
        hit = ids[slot][None, :] == expert
        named = named + jnp.where(hit, 1.0, 0.0)
        gate = gate + jnp.where(hit, probs[slot][None, :], 0.0)
    before = lax.broadcasted_iota(jnp.int32, (tokens, tokens), 0)
    after = lax.broadcasted_iota(jnp.int32, (tokens, tokens), 1)
    earlier = mm(named.astype(BF16), (before < after).astype(BF16), 1, 0)
    place = (row % CAP).astype(F32)
    pick = (named > 0.5) & (earlier == place)
    return pick, jnp.where(pick, gate, 0.0), row % (2 * CAP) < CAP


def local(latent, expert_ids, gate_probs, cotangent, w_gate_up, w_down):
    tokens, lat = latent.shape
    top = expert_ids.shape[1]
    columns = lax.axis_size("expert")
    replicas = lax.axis_size("dp")
    weight_in = w_gate_up[0]
    weight_out = w_down[0]
    ffw = weight_out.shape[1]
    slots = columns * CAP

    pick, gate, first = route(expert_ids, gate_probs, columns)
    token_part = jnp.where(pick & first, 1.0, 0.0).astype(BF16)
    gate_part = jnp.where(first, 0.0, gate)
    gate_high, gate_low = halves(gate_part)
    sent = mm(
        jnp.concatenate([token_part, gate_high, gate_low], axis=1),
        jnp.concatenate([latent, cotangent, cotangent], axis=0), 1, 0,
    ).astype(BF16)
    there = lax.all_to_all(
        sent.reshape(columns, 2 * CAP, lat), "expert", split_axis=0, concat_axis=0, tiled=True
    )
    rows = there[:, :CAP].reshape(slots, lat)
    cot = there[:, CAP:].reshape(slots, lat)

    hidden = mm(rows, weight_in, 1, 0)
    g = hidden[:, :ffw]
    u = hidden[:, ffw:]
    s = jax.nn.sigmoid(g)
    act = (g * s * u).astype(BF16)
    out = mm(act, weight_out, 1, 1).astype(BF16)
    grad_act = mm(cot, weight_out, 1, 0)
    grad_hidden = jnp.concatenate(
        [grad_act * u * s * (1.0 + g * (1.0 - s)), grad_act * g * s], axis=1
    ).astype(BF16)
    grad_rows = mm(grad_hidden, weight_in, 1, 1).astype(BF16)
    back = lax.all_to_all(
        jnp.concatenate(
            [out.reshape(columns, CAP, lat), grad_rows.reshape(columns, CAP, lat)], axis=1
        ),
        "expert", split_axis=0, concat_axis=0, tiled=True,
    )

    terms = jnp.concatenate([mm(rows, grad_hidden, 0, 0), mm(cot, act, 0, 0)], axis=1)
    width = 3 * ffw
    share = lat // replicas
    terms = terms.astype(BF16).reshape(replicas // 2, 2, share, width)
    core = lax.axis_index("dp") % 2
    mine = jnp.where(core == 0, terms[:, 0], terms[:, 1])
    other = jnp.where(core == 0, terms[:, 1], terms[:, 0])
    swapped = lax.ppermute(other, "dp", [(i, i ^ 1) for i in range(replicas)])
    pair = (mine.astype(F32) + swapped.astype(F32)).astype(BF16).reshape(lat // 2, width)
    summed = lax.psum_scatter(
        pair, "dp", scatter_dimension=0, tiled=True,
        axis_index_groups=[list(range(c, replicas, 2)) for c in range(2)],
    )

    home = back.reshape(2 * slots, lat)
    out_high, out_low = halves(jnp.where(pick & first, gate, 0.0))
    mixed = (mm(out_high, home, 0, 0) + mm(out_low, home, 0, 0)).astype(BF16)
    latent_gradient = mm(jnp.where(pick & ~first, 1.0, 0.0).astype(BF16), home, 0, 0).astype(BF16)
    inner = mm(home, cotangent, 1, 1)
    inner = jnp.where(pick & first, inner, 0.0)
    row = lax.broadcasted_iota(jnp.int32, inner.shape, 0)
    expert = row // (2 * CAP) * EXP_DEV
    ids = expert_ids.T
    gate_grad = jnp.stack(
        [jnp.sum(jnp.where(ids[k][None, :] == expert, inner, 0.0), axis=0) for k in range(top)], axis=1
    )
    return (mixed, latent_gradient, gate_grad, summed[None, :, : 2 * ffw], summed[None, :, 2 * ffw :])


def solution(mesh):
    return jax.shard_map(
        local,
        mesh=mesh,
        in_specs=(
            P(("dp", "expert"), None),
            P(("dp", "expert"), None),
            P(("dp", "expert"), None),
            P(("dp", "expert"), None),
            P("expert", None, None),
            P("expert", None, None),
        ),
        out_specs=(
            P(("dp", "expert"), None),
            P(("dp", "expert"), None),
            P(("dp", "expert"), None),
            P("expert", "dp", None),
            P("expert", "dp", None),
        ),
        check_vma=False,
    )
```

```python
import jax
import jax.numpy as jnp
from jax import lax
from jax.experimental import pallas as pl
from jax.experimental.pallas import tpu as pltpu
from jax.sharding import PartitionSpec as P

EXP_DEV = 4
CAP = 2
GROUP = 4 * CAP
F32 = jnp.float32
BF16 = jnp.bfloat16
VMEM_BYTES = 48 << 20


def mm(a, b, ca=1, cb=0):
    return lax.dot_general(a, b, (((ca,), (cb,)), ((), ())), preferred_element_type=F32)


def iota(shape, dim):
    return lax.broadcasted_iota(jnp.int32, shape, dim)


def halves(value):
    high = value.astype(BF16)
    return high, (value - high.astype(F32)).astype(BF16)


def routing(ids_ref, probs_ref, rows):
    tokens = ids_ref.shape[1]
    row = iota((rows, tokens), 0)
    expert = (row // GROUP) * EXP_DEV
    named = jnp.zeros((rows, tokens), F32)
    gate = jnp.zeros((rows, tokens), F32)
    for slot in range(ids_ref.shape[0]):
        hit = ids_ref[slot : slot + 1, :] == expert
        named = jnp.where(hit, 1.0, named)
        gate = jnp.where(hit, probs_ref[slot : slot + 1, :], gate)
    before = iota((tokens, tokens), 0)
    after = iota((tokens, tokens), 1)
    earlier = mm(named.astype(BF16), jnp.where(before < after, 1.0, 0.0).astype(BF16))
    pick = (named > 0.5) & (earlier == (row & 1).astype(F32))
    kind = (row & 2) == 0
    half = (row & 4) == 0
    return pick, gate, kind, half, expert


def zero_one(mask):
    return jnp.where(mask, 1.0, 0.0).astype(BF16)


def pack_kernel(ids_ref, probs_ref, latent_ref, cot_ref, sent_ref):
    rows, wide = sent_ref.shape
    pick, gate, first, low, _ = routing(ids_ref, probs_ref, rows)
    token = jnp.where(pick & first, 1.0, 0.0)
    weight = jnp.where(pick & ~first, gate, 0.0)
    total = jnp.zeros((rows, wide), F32)
    for h in range(2):
        here = low if h == 0 else ~low
        high, rest = halves(jnp.where(here, weight, 0.0))
        picks = jnp.concatenate([jnp.where(here, token, 0.0).astype(BF16), high, rest], axis=1)
        cols = pl.ds(h * wide, wide)
        cot = cot_ref[:, cols]
        total = total + mm(picks, jnp.concatenate([latent_ref[:, cols], cot, cot], axis=0))
    sent_ref[...] = total.astype(BF16)


def sorted_position(index, slots):
    group = index // GROUP
    return ((index & 2) + ((index >> 2) & 1)) * slots + group * CAP + (index & 1)


def expert_kernel(core_ref, there_ref, win_ref, wout_ref, back_ref, mine_ref, other_ref, terms_ref):
    rows, wide = there_ref.shape
    slots = rows // 4
    ffw = wout_ref.shape[1]
    share = mine_ref.shape[1]
    sort = zero_one(iota((rows, rows), 0) == sorted_position(iota((rows, rows), 1), slots))
    data = mm(sort, there_ref[...]).astype(BF16)
    vec = [data[:slots], data[slots : 2 * slots]]
    cot = [data[2 * slots : 3 * slots], data[3 * slots :]]
    top = [pl.ds(0, wide), pl.ds(wide, wide)]

    hidden = mm(vec[0], win_ref[top[0], :]) + mm(vec[1], win_ref[top[1], :])
    g = hidden[:, :ffw]
    u = hidden[:, ffw:]
    s = 1.0 / (1.0 + jnp.exp(-g))
    act = (g * s * u).astype(BF16)
    grad_act = mm(cot[0], wout_ref[top[0], :]) + mm(cot[1], wout_ref[top[1], :])
    grad_hidden = jnp.concatenate(
        [grad_act * u * s * (1.0 + g * (1.0 - s)), grad_act * g * s], axis=1
    ).astype(BF16)

    for h in range(2):
        terms_ref[top[h], : 2 * ffw] = mm(vec[h], grad_hidden, 0, 0).astype(BF16)
        terms_ref[top[h], 2 * ffw :] = mm(cot[h], act, 0, 0).astype(BF16)
    even = core_ref[0] == 0
    for block in range(mine_ref.shape[0]):
        a = terms_ref[pl.ds(2 * block * share, share), :]
        b = terms_ref[pl.ds((2 * block + 1) * share, share), :]
        mine_ref[block] = jnp.where(even, a, b)
        other_ref[block] = jnp.where(even, b, a)

    result = jnp.concatenate(
        [mm(act, wout_ref[top[h], :], 1, 1).astype(BF16) for h in range(2)]
        + [mm(grad_hidden, win_ref[top[h], :], 1, 1).astype(BF16) for h in range(2)],
        axis=0,
    )
    unsort = zero_one(iota((rows, rows), 1) == sorted_position(iota((rows, rows), 0), slots))
    back_ref[...] = mm(unsort, result).astype(BF16)


def add_kernel(a_ref, b_ref, out_ref):
    out_ref[...] = (a_ref[...].astype(F32) + b_ref[...].astype(F32)).astype(BF16)


def combine_kernel(ids_ref, probs_ref, cot_ref, home_ref, mixed_ref, latgrad_ref, gate_ref):
    rows, wide = home_ref.shape
    pick, gate, first, low, expert = routing(ids_ref, probs_ref, rows)
    home = home_ref[...]
    chosen = pick & first
    weight = jnp.where(chosen, gate, 0.0)
    token = jnp.where(pick & ~first, 1.0, 0.0)
    inner = jnp.zeros(weight.shape, F32)
    for h in range(2):
        here = low if h == 0 else ~low
        cols = pl.ds(h * wide, wide)
        high, rest = halves(jnp.where(here, weight, 0.0))
        mixed_ref[:, cols] = (mm(high, home, 0, 0) + mm(rest, home, 0, 0)).astype(BF16)
        latgrad_ref[:, cols] = mm(jnp.where(here, token, 0.0).astype(BF16), home, 0, 0).astype(BF16)
        inner = jnp.where(here & chosen, mm(home, cot_ref[:, cols], 1, 1), inner)
    for slot in range(ids_ref.shape[0]):
        hit = ids_ref[slot : slot + 1, :] == expert
        gate_ref[slot : slot + 1, :] = jnp.sum(jnp.where(hit, inner, 0.0), axis=0, keepdims=True)


def call(kernel, outs, scratch=(), specs=None):
    shapes = [jax.ShapeDtypeStruct(shape, dtype) for shape, dtype in outs]
    return pl.pallas_call(
        kernel,
        out_shape=shapes,
        in_specs=specs,
        out_specs=[pl.BlockSpec(memory_space=pltpu.VMEM)] * len(shapes),
        scratch_shapes=list(scratch),
        compiler_params=pltpu.CompilerParams(vmem_limit_bytes=VMEM_BYTES),
        name=kernel.__name__,
    )


def local(latent, expert_ids, gate_probs, cotangent, w_gate_up, w_down):
    tokens, lat = latent.shape
    top = expert_ids.shape[1]
    columns = lax.axis_size("expert")
    replicas = lax.axis_size("dp")
    ffw = w_down.shape[2]
    rows = columns * GROUP
    wide = lat // 2
    width = 3 * ffw
    share = lat // replicas
    ids = expert_ids.T
    probs = gate_probs.T
    vmem = pl.BlockSpec(memory_space=pltpu.VMEM)

    (sent,) = call(pack_kernel, [((rows, wide), BF16)], specs=[vmem] * 4)(ids, probs, latent, cotangent)
    there = exchange(sent, columns)

    core = (lax.axis_index("dp") % 2).astype(jnp.int32).reshape(1)
    half_terms = ((replicas // 2, share, width), BF16)
    back, mine, other = call(
        expert_kernel,
        [((rows, wide), BF16), half_terms, half_terms],
        scratch=[pltpu.VMEM((lat, width), BF16)],
        specs=[pl.BlockSpec(memory_space=pltpu.SMEM)] + [vmem] * 3,
    )(core, there, w_gate_up[0], w_down[0])

    swapped = lax.ppermute(other, "dp", [(i, i ^ 1) for i in range(replicas)])
    (pair,) = call(add_kernel, [half_terms], specs=[vmem] * 2)(mine, swapped)
    pair, back = lax.optimization_barrier((pair, back))
    summed = lax.psum_scatter(
        pair.reshape(lat // 2, width), "dp", scatter_dimension=0, tiled=True,
        axis_index_groups=[list(range(c, replicas, 2)) for c in range(2)],
    )
    home = exchange(back, columns)
    mixed, latent_gradient, gate_grad = call(
        combine_kernel,
        [((tokens, lat), BF16), ((tokens, lat), BF16), ((top, tokens), F32)],
        specs=[vmem] * 4,
    )(ids, probs, cotangent, home)
    return (
        mixed, latent_gradient, gate_grad.T, summed[None, :, : 2 * ffw], summed[None, :, 2 * ffw :]
    )


def exchange(message, columns):
    rows, wide = message.shape
    moved = lax.all_to_all(
        message.reshape(columns, rows // columns, wide), "expert", split_axis=0, concat_axis=0, tiled=True
    )
    return moved.reshape(rows, wide)


def solution(mesh):
    return jax.shard_map(
        local,
        mesh=mesh,
        in_specs=(
            P(("dp", "expert"), None),
            P(("dp", "expert"), None),
            P(("dp", "expert"), None),
            P(("dp", "expert"), None),
            P("expert", None, None),
            P("expert", None, None),
        ),
        out_specs=(
            P(("dp", "expert"), None),
            P(("dp", "expert"), None),
            P(("dp", "expert"), None),
            P("expert", "dp", None),
            P("expert", "dp", None),
        ),
        check_vma=False,
    )
```

```python
import jax
import jax.numpy as jnp
from jax import lax
from jax.experimental import pallas as pl
from jax.experimental.pallas import tpu as pltpu
from jax.sharding import PartitionSpec as P

EXP_DEV = 4
CAP = 2
GROUP = 4 * CAP
F32 = jnp.float32
BF16 = jnp.bfloat16
VMEM_BYTES = 48 << 20
ALL_VMEM_BYTES = 63 << 20


def mm(a, b, ca=1, cb=0):
    return lax.dot_general(a, b, (((ca,), (cb,)), ((), ())), preferred_element_type=F32)


def iota(shape, dim):
    return lax.broadcasted_iota(jnp.int32, shape, dim)


def halves(value):
    high = value.astype(BF16)
    return high, (value - high.astype(F32)).astype(BF16)


def routing(ids_ref, probs_ref, rows):
    tokens = ids_ref.shape[1]
    row = iota((rows, tokens), 0)
    expert = (row // GROUP) * EXP_DEV
    named = jnp.zeros((rows, tokens), F32)
    gate = jnp.zeros((rows, tokens), F32)
    for slot in range(ids_ref.shape[0]):
        hit = ids_ref[slot : slot + 1, :] == expert
        named = jnp.where(hit, 1.0, named)
        gate = jnp.where(hit, probs_ref[slot : slot + 1, :], gate)
    before = iota((tokens, tokens), 0)
    after = iota((tokens, tokens), 1)
    earlier = mm(named.astype(BF16), jnp.where(before < after, 1.0, 0.0).astype(BF16))
    pick = (named > 0.5) & (earlier == (row & 1).astype(F32))
    kind = (row & 2) == 0
    half = (row & 4) == 0
    return pick, gate, kind, half, expert


def zero_one(mask):
    return jnp.where(mask, 1.0, 0.0).astype(BF16)


def pack_kernel(ids_hbm, probs_hbm, latent_hbm, cot_hbm, sent_ref, ids_ref, probs_ref, latent_ref, cot_ref, sems):
    rows, wide = sent_ref.shape
    pairs = [(ids_hbm, ids_ref), (probs_hbm, probs_ref), (latent_hbm, latent_ref), (cot_hbm, cot_ref)]
    copies = [pltpu.make_async_copy(a, b, sems.at[i]) for i, (a, b) in enumerate(pairs)]
    for copy in copies:
        copy.start()
    copies[0].wait()
    copies[1].wait()
    pick, gate, first, low, _ = routing(ids_ref, probs_ref, rows)
    token = jnp.where(pick & first, 1.0, 0.0)
    weight = jnp.where(pick & ~first, gate, 0.0)
    copies[2].wait()
    copies[3].wait()
    total = jnp.zeros((rows, wide), F32)
    for h in range(2):
        here = low if h == 0 else ~low
        high, rest = halves(jnp.where(here, weight, 0.0))
        picks = jnp.concatenate([jnp.where(here, token, 0.0).astype(BF16), high, rest], axis=1)
        cols = pl.ds(h * wide, wide)
        cot = cot_ref[:, cols]
        total = total + mm(picks, jnp.concatenate([latent_ref[:, cols], cot, cot], axis=0))
    sent_ref[...] = total.astype(BF16)


def sorted_position(index, slots):
    group = index // GROUP
    return ((index & 2) + ((index >> 2) & 1)) * slots + group * CAP + (index & 1)


def expert_kernel(
    core_ref, there_ref, win_ref, wout_ref, mine_ref, other_ref, act_ref, grad_ref, terms_ref
):
    rows, wide = there_ref.shape
    slots = rows // 4
    ffw = wout_ref.shape[1]
    share = mine_ref.shape[1]
    sort = zero_one(iota((rows, rows), 0) == sorted_position(iota((rows, rows), 1), slots))
    data = mm(sort, there_ref[...]).astype(BF16)
    vec = [data[:slots], data[slots : 2 * slots]]
    cot = [data[2 * slots : 3 * slots], data[3 * slots :]]
    top = [pl.ds(0, wide), pl.ds(wide, wide)]

    hidden = mm(vec[0], win_ref[top[0], :]) + mm(vec[1], win_ref[top[1], :])
    g = hidden[:, :ffw]
    u = hidden[:, ffw:]
    s = 1.0 / (1.0 + jnp.exp(-g))
    act = (g * s * u).astype(BF16)
    grad_act = mm(cot[0], wout_ref[top[0], :]) + mm(cot[1], wout_ref[top[1], :])
    grad_hidden = jnp.concatenate(
        [grad_act * u * s * (1.0 + g * (1.0 - s)), grad_act * g * s], axis=1
    ).astype(BF16)
    act_ref[...] = act
    grad_ref[...] = grad_hidden

    for h in range(2):
        terms_ref[top[h], : 2 * ffw] = mm(vec[h], grad_hidden, 0, 0).astype(BF16)
        terms_ref[top[h], 2 * ffw :] = mm(cot[h], act, 0, 0).astype(BF16)
    even = core_ref[0] == 0
    for block in range(mine_ref.shape[0]):
        a = terms_ref[pl.ds(2 * block * share, share), :]
        b = terms_ref[pl.ds((2 * block + 1) * share, share), :]
        mine_ref[block] = jnp.where(even, a, b)
        other_ref[block] = jnp.where(even, b, a)


def return_kernel(act_ref, grad_ref, win_ref, wout_ref, back_ref):
    rows, wide = back_ref.shape
    slots = rows // 4
    top = [pl.ds(0, wide), pl.ds(wide, wide)]
    act = act_ref[...]
    grad_hidden = grad_ref[...]
    result = jnp.concatenate(
        [mm(act, wout_ref[top[h], :], 1, 1).astype(BF16) for h in range(2)]
        + [mm(grad_hidden, win_ref[top[h], :], 1, 1).astype(BF16) for h in range(2)],
        axis=0,
    )
    unsort = zero_one(iota((rows, rows), 1) == sorted_position(iota((rows, rows), 0), slots))
    back_ref[...] = mm(unsort, result).astype(BF16)


def split_kernel(sum_hbm, gate_up_ref, down_ref, sems):
    cut = gate_up_ref.shape[1]
    copies = [
        pltpu.make_async_copy(sum_hbm.at[:, pl.ds(0, cut)], gate_up_ref, sems.at[0]),
        pltpu.make_async_copy(sum_hbm.at[:, pl.ds(cut, down_ref.shape[1])], down_ref, sems.at[1]),
    ]
    for copy in copies:
        copy.start()
    for copy in copies:
        copy.wait()


def add_kernel(a_ref, b_ref, out_ref):
    out_ref[...] = (a_ref[...].astype(F32) + b_ref[...].astype(F32)).astype(BF16)


def mask_kernel(ids_ref, probs_ref, pick_ref, weight_ref):
    pick, gate, first, _, _ = routing(ids_ref, probs_ref, weight_ref.shape[0])
    pick_ref[...] = zero_one(pick)
    weight_ref[...] = jnp.where(pick & first, gate, 0.0)


def combine_kernel(ids_ref, pick_ref, weight_ref, cot_ref, home_ref, mixed_ref, latgrad_ref, gate_ref):
    rows, wide = home_ref.shape
    weight = weight_ref[...]
    pick = pick_ref[...].astype(F32)
    row = iota(weight.shape, 0)
    expert = (row // GROUP) * EXP_DEV
    first = (row & 2) == 0
    low = (row & 4) == 0
    home = home_ref[...]
    chosen = jnp.where(first, pick, 0.0)
    token = pick - chosen
    inner = jnp.zeros(weight.shape, F32)
    for h in range(2):
        here = low if h == 0 else ~low
        cols = pl.ds(h * wide, wide)
        high, rest = halves(jnp.where(here, weight, 0.0))
        mixed_ref[:, cols] = (mm(high, home, 0, 0) + mm(rest, home, 0, 0)).astype(BF16)
        latgrad_ref[:, cols] = mm(jnp.where(here, token, 0.0).astype(BF16), home, 0, 0).astype(BF16)
        inner = jnp.where(here, mm(home, cot_ref[:, cols], 1, 1), inner)
    inner = jnp.where(chosen > 0.5, inner, 0.0)
    for slot in range(ids_ref.shape[0]):
        hit = ids_ref[slot : slot + 1, :] == expert
        gate_ref[slot : slot + 1, :] = jnp.sum(jnp.where(hit, inner, 0.0), axis=0, keepdims=True)


def call(kernel, outs, scratch=(), specs=None, vmem=VMEM_BYTES):
    shapes = [jax.ShapeDtypeStruct(shape, dtype) for shape, dtype in outs]
    return pl.pallas_call(
        kernel,
        out_shape=shapes,
        in_specs=specs,
        out_specs=[pl.BlockSpec(memory_space=pltpu.VMEM)] * len(shapes),
        scratch_shapes=list(scratch),
        compiler_params=pltpu.CompilerParams(vmem_limit_bytes=vmem),
        name=kernel.__name__,
    )


def local(latent, expert_ids, gate_probs, cotangent, w_gate_up, w_down):
    tokens, lat = latent.shape
    top = expert_ids.shape[1]
    columns = lax.axis_size("expert")
    replicas = lax.axis_size("dp")
    ffw = w_down.shape[2]
    rows = columns * GROUP
    wide = lat // 2
    width = 3 * ffw
    share = lat // replicas
    ids = expert_ids.T
    probs = gate_probs.T
    vmem = pl.BlockSpec(memory_space=pltpu.VMEM)

    (sent,) = call(
        pack_kernel,
        [((rows, wide), BF16)],
        scratch=[pltpu.VMEM(a.shape, a.dtype) for a in (ids, probs, latent, cotangent)]
        + [pltpu.SemaphoreType.DMA((4,))],
        specs=[pl.BlockSpec(memory_space=pl.ANY)] * 4,
        vmem=ALL_VMEM_BYTES,
    )(ids, probs, latent, cotangent)
    there = exchange(sent, columns)

    core = (lax.axis_index("dp") % 2).astype(jnp.int32).reshape(1)
    half_terms = ((replicas // 2, share, width), BF16)
    slots = columns * CAP
    mine, other, act, grad_hidden = call(
        expert_kernel,
        [half_terms, half_terms, ((slots, ffw), BF16), ((slots, 2 * ffw), BF16)],
        scratch=[pltpu.VMEM((lat, width), BF16)],
        specs=[pl.BlockSpec(memory_space=pltpu.SMEM)] + [vmem] * 3,
    )(core, there, w_gate_up[0], w_down[0])

    swapped = lax.ppermute(other, "dp", [(i, i ^ 1) for i in range(replicas)])
    (back,) = call(return_kernel, [((rows, wide), BF16)], specs=[vmem] * 4)(
        act, grad_hidden, w_gate_up[0], w_down[0]
    )
    (pair,) = call(add_kernel, [half_terms], specs=[vmem] * 2)(mine, swapped)
    pair, back = lax.optimization_barrier((pair, back))
    summed = lax.psum_scatter(
        pair.reshape(lat // 2, width), "dp", scatter_dimension=0, tiled=True,
        axis_index_groups=[list(range(c, replicas, 2)) for c in range(2)],
    )
    home = lax.cond(core[0] < 2, lambda b: exchange(b, columns), lambda b: b, back)
    pick, weight = call(
        mask_kernel, [((rows, tokens), BF16), ((rows, tokens), F32)], specs=[vmem] * 2
    )(ids, probs)
    mixed, latent_gradient, gate_grad = call(
        combine_kernel,
        [((tokens, lat), BF16), ((tokens, lat), BF16), ((top, tokens), F32)],
        specs=[vmem] * 5,
    )(ids, pick, weight, cotangent, home)
    summed, mixed, latent_gradient, gate_grad = lax.optimization_barrier(
        (summed, mixed, latent_gradient, gate_grad)
    )
    gate_up_grad, down_grad = call(
        split_kernel,
        [((share, 2 * ffw), BF16), ((share, ffw), BF16)],
        scratch=[pltpu.SemaphoreType.DMA((2,))],
        specs=[pl.BlockSpec(memory_space=pl.ANY)],
        vmem=ALL_VMEM_BYTES,
    )(summed)
    return (mixed, latent_gradient, gate_grad.T, gate_up_grad[None], down_grad[None])


def exchange(message, columns):
    rows, wide = message.shape
    moved = lax.all_to_all(
        message.reshape(columns, rows // columns, wide), "expert", split_axis=0, concat_axis=0, tiled=True
    )
    return moved.reshape(rows, wide)


def solution(mesh):
    return jax.shard_map(
        local,
        mesh=mesh,
        in_specs=(
            P(("dp", "expert"), None),
            P(("dp", "expert"), None),
            P(("dp", "expert"), None),
            P(("dp", "expert"), None),
            P("expert", None, None),
            P("expert", None, None),
        ),
        out_specs=(
            P(("dp", "expert"), None),
            P(("dp", "expert"), None),
            P(("dp", "expert"), None),
            P("expert", "dp", None),
            P("expert", "dp", None),
        ),
        check_vma=False,
    )
```

```python
import jax
import jax.numpy as jnp
from jax import lax
from jax.experimental import pallas as pl
from jax.experimental.pallas import tpu as pltpu
from jax.sharding import PartitionSpec as P

EXP_DEV = 4
CAP = 2
GROUP = 4 * CAP
RING = 4
F32 = jnp.float32
BF16 = jnp.bfloat16
VMEM_BYTES = 48 << 20
ALL_VMEM_BYTES = 63 << 20


def mm(a, b, ca=1, cb=0):
    return lax.dot_general(a, b, (((ca,), (cb,)), ((), ())), preferred_element_type=F32)


def iota(shape, dim):
    return lax.broadcasted_iota(jnp.int32, shape, dim)


def halves(value):
    high = value.astype(BF16)
    return high, (value - high.astype(F32)).astype(BF16)


def leaving(row, rows):
    part = rows // RING
    return row // part, (row % part) // GROUP


def arriving(row):
    piece = (row // GROUP) % RING
    step = jnp.where(piece == 0, 0, jnp.where(piece == 1, RING - 1, piece - 1))
    return step, row // (GROUP * RING)


def expert_id(step, place, plane, rows):
    return (((plane + step) % RING) * (rows // (GROUP * RING)) + place) * EXP_DEV


def routing(ids_ref, probs_ref, expert):
    rows, tokens = expert.shape
    row = iota((rows, tokens), 0)
    named = jnp.zeros((rows, tokens), F32)
    gate = jnp.zeros((rows, tokens), F32)
    for slot in range(ids_ref.shape[0]):
        hit = ids_ref[slot : slot + 1, :] == expert
        named = jnp.where(hit, 1.0, named)
        gate = jnp.where(hit, probs_ref[slot : slot + 1, :], gate)
    before = iota((tokens, tokens), 0)
    after = iota((tokens, tokens), 1)
    earlier = mm(named.astype(BF16), jnp.where(before < after, 1.0, 0.0).astype(BF16))
    pick = (named > 0.5) & (earlier == (row & 1).astype(F32))
    kind = (row & 2) == 0
    half = (row & 4) == 0
    return pick, gate, kind, half


def zero_one(mask):
    return jnp.where(mask, 1.0, 0.0).astype(BF16)


def store_leaving(message, stay_ref, right_ref, left_ref):
    part = stay_ref.shape[0]
    middle = 2 * part + part // 2
    stay_ref[...] = message[:part]
    right_ref[...] = message[part:middle]
    left_ref[...] = message[middle:]


def pack_kernel(
    plane_ref, ids_hbm, probs_hbm, latent_hbm, cot_hbm, stay_ref, right_ref, left_ref,
    ids_ref, probs_ref, latent_ref, cot_ref, sems
):
    part, wide = stay_ref.shape
    rows = RING * part
    pairs = [(ids_hbm, ids_ref), (probs_hbm, probs_ref), (latent_hbm, latent_ref), (cot_hbm, cot_ref)]
    copies = [pltpu.make_async_copy(a, b, sems.at[i]) for i, (a, b) in enumerate(pairs)]
    for copy in copies:
        copy.start()
    copies[0].wait()
    copies[1].wait()
    step, place = leaving(iota((rows, ids_ref.shape[1]), 0), rows)
    expert = expert_id(step, place, plane_ref[0], rows)
    pick, gate, first, low = routing(ids_ref, probs_ref, expert)
    token = jnp.where(pick & first, 1.0, 0.0)
    weight = jnp.where(pick & ~first, gate, 0.0)
    copies[2].wait()
    copies[3].wait()
    total = jnp.zeros((rows, wide), F32)
    for h in range(2):
        here = low if h == 0 else ~low
        high, rest = halves(jnp.where(here, weight, 0.0))
        picks = jnp.concatenate([jnp.where(here, token, 0.0).astype(BF16), high, rest], axis=1)
        cols = pl.ds(h * wide, wide)
        cot = cot_ref[:, cols]
        total = total + mm(picks, jnp.concatenate([latent_ref[:, cols], cot, cot], axis=0))
    store_leaving(total.astype(BF16), stay_ref, right_ref, left_ref)


def sorted_position(index, slots):
    group = index // GROUP
    return ((index & 2) + ((index >> 2) & 1)) * slots + group * CAP + (index & 1)


def expert_kernel(
    core_ref, there_ref, win_ref, wout_ref, mine_ref, other_ref, act_ref, grad_ref, terms_ref
):
    rows, wide = there_ref.shape
    slots = rows // 4
    ffw = wout_ref.shape[1]
    share = mine_ref.shape[1]
    sort = zero_one(iota((rows, rows), 0) == sorted_position(iota((rows, rows), 1), slots))
    data = mm(sort, there_ref[...]).astype(BF16)
    vec = [data[:slots], data[slots : 2 * slots]]
    cot = [data[2 * slots : 3 * slots], data[3 * slots :]]
    top = [pl.ds(0, wide), pl.ds(wide, wide)]

    hidden = mm(vec[0], win_ref[top[0], :]) + mm(vec[1], win_ref[top[1], :])
    g = hidden[:, :ffw]
    u = hidden[:, ffw:]
    s = 1.0 / (1.0 + jnp.exp(-g))
    act = (g * s * u).astype(BF16)
    grad_act = mm(cot[0], wout_ref[top[0], :]) + mm(cot[1], wout_ref[top[1], :])
    grad_hidden = jnp.concatenate(
        [grad_act * u * s * (1.0 + g * (1.0 - s)), grad_act * g * s], axis=1
    ).astype(BF16)
    act_ref[...] = act
    grad_ref[...] = grad_hidden

    for h in range(2):
        terms_ref[top[h], : 2 * ffw] = mm(vec[h], grad_hidden, 0, 0).astype(BF16)
        terms_ref[top[h], 2 * ffw :] = mm(cot[h], act, 0, 0).astype(BF16)
    even = core_ref[0] == 0
    for block in range(mine_ref.shape[0]):
        a = terms_ref[pl.ds(2 * block * share, share), :]
        b = terms_ref[pl.ds((2 * block + 1) * share, share), :]
        mine_ref[block] = jnp.where(even, a, b)
        other_ref[block] = jnp.where(even, b, a)


def return_kernel(act_ref, grad_ref, win_ref, wout_ref, stay_ref, right_ref, left_ref):
    part, wide = stay_ref.shape
    rows = RING * part
    slots = rows // 4
    top = [pl.ds(0, wide), pl.ds(wide, wide)]
    act = act_ref[...]
    grad_hidden = grad_ref[...]
    result = jnp.concatenate(
        [mm(act, wout_ref[top[h], :], 1, 1).astype(BF16) for h in range(2)]
        + [mm(grad_hidden, win_ref[top[h], :], 1, 1).astype(BF16) for h in range(2)],
        axis=0,
    )
    row = iota((rows, rows), 0)
    step, place = leaving(row, rows)
    piece = jnp.where(step == 0, 0, jnp.where(step == RING - 1, 1, step + 1))
    source = (place * RING + piece) * GROUP + row % GROUP
    unsort = zero_one(iota((rows, rows), 1) == sorted_position(source, slots))
    store_leaving(mm(unsort, result).astype(BF16), stay_ref, right_ref, left_ref)


def split_kernel(sum_hbm, gate_up_ref, down_ref, sems):
    cut = gate_up_ref.shape[1]
    copies = [
        pltpu.make_async_copy(sum_hbm.at[:, pl.ds(0, cut)], gate_up_ref, sems.at[0]),
        pltpu.make_async_copy(sum_hbm.at[:, pl.ds(cut, down_ref.shape[1])], down_ref, sems.at[1]),
    ]
    for copy in copies:
        copy.start()
    for copy in copies:
        copy.wait()


def add_kernel(a_ref, b_ref, out_ref):
    out_ref[...] = (a_ref[...].astype(F32) + b_ref[...].astype(F32)).astype(BF16)


def mask_kernel(plane_ref, ids_ref, probs_ref, pick_ref, weight_ref):
    step, place = arriving(iota(weight_ref.shape, 0))
    expert = expert_id(step, place, plane_ref[0], weight_ref.shape[0])
    pick, gate, first, _ = routing(ids_ref, probs_ref, expert)
    pick_ref[...] = zero_one(pick)
    weight_ref[...] = jnp.where(pick & first, gate, 0.0)


def combine_kernel(plane_ref, ids_ref, pick_ref, weight_ref, cot_ref, home_ref, mixed_ref, latgrad_ref, gate_ref):
    rows, wide = home_ref.shape
    weight = weight_ref[...]
    pick = pick_ref[...].astype(F32)
    row = iota(weight.shape, 0)
    step, place = arriving(row)
    expert = expert_id(step, place, plane_ref[0], rows)
    first = (row & 2) == 0
    low = (row & 4) == 0
    home = home_ref[...]
    chosen = jnp.where(first, pick, 0.0)
    token = pick - chosen
    inner = jnp.zeros(weight.shape, F32)
    for h in range(2):
        here = low if h == 0 else ~low
        cols = pl.ds(h * wide, wide)
        high, rest = halves(jnp.where(here, weight, 0.0))
        mixed_ref[:, cols] = (mm(high, home, 0, 0) + mm(rest, home, 0, 0)).astype(BF16)
        latgrad_ref[:, cols] = mm(jnp.where(here, token, 0.0).astype(BF16), home, 0, 0).astype(BF16)
        inner = jnp.where(here, mm(home, cot_ref[:, cols], 1, 1), inner)
    inner = jnp.where(chosen > 0.5, inner, 0.0)
    for slot in range(ids_ref.shape[0]):
        hit = ids_ref[slot : slot + 1, :] == expert
        gate_ref[slot : slot + 1, :] = jnp.sum(jnp.where(hit, inner, 0.0), axis=0, keepdims=True)


def call(kernel, outs, scratch=(), specs=None, vmem=VMEM_BYTES):
    shapes = [jax.ShapeDtypeStruct(shape, dtype) for shape, dtype in outs]
    return pl.pallas_call(
        kernel,
        out_shape=shapes,
        in_specs=specs,
        out_specs=[pl.BlockSpec(memory_space=pltpu.VMEM)] * len(shapes),
        scratch_shapes=list(scratch),
        compiler_params=pltpu.CompilerParams(vmem_limit_bytes=vmem),
        name=kernel.__name__,
    )


def local(latent, expert_ids, gate_probs, cotangent, w_gate_up, w_down):
    tokens, lat = latent.shape
    top = expert_ids.shape[1]
    columns = lax.axis_size("expert")
    replicas = lax.axis_size("dp")
    ffw = w_down.shape[2]
    rows = columns * GROUP
    wide = lat // 2
    width = 3 * ffw
    share = lat // replicas
    ids = expert_ids.T
    probs = gate_probs.T
    vmem = pl.BlockSpec(memory_space=pltpu.VMEM)

    smem = pl.BlockSpec(memory_space=pltpu.SMEM)
    plane = (lax.axis_index("expert") // (columns // RING)).astype(jnp.int32).reshape(1)
    part = rows // RING
    leave = [((part, wide), BF16), ((part + part // 2, wide), BF16), ((part + part // 2, wide), BF16)]

    sent = call(
        pack_kernel,
        leave,
        scratch=[pltpu.VMEM(a.shape, a.dtype) for a in (ids, probs, latent, cotangent)]
        + [pltpu.SemaphoreType.DMA((4,))],
        specs=[smem] + [pl.BlockSpec(memory_space=pl.ANY)] * 4,
        vmem=ALL_VMEM_BYTES,
    )(plane, ids, probs, latent, cotangent)
    there = exchange(*sent)

    core = (lax.axis_index("dp") % 2).astype(jnp.int32).reshape(1)
    half_terms = ((replicas // 2, share, width), BF16)
    slots = columns * CAP
    mine, other, act, grad_hidden = call(
        expert_kernel,
        [half_terms, half_terms, ((slots, ffw), BF16), ((slots, 2 * ffw), BF16)],
        scratch=[pltpu.VMEM((lat, width), BF16)],
        specs=[smem] + [vmem] * 3,
    )(core, there, w_gate_up[0], w_down[0])

    swapped = lax.ppermute(other, "dp", [(i, i ^ 1) for i in range(replicas)])
    back = call(return_kernel, leave, specs=[vmem] * 4)(
        act, grad_hidden, w_gate_up[0], w_down[0]
    )
    (pair,) = call(add_kernel, [half_terms], specs=[vmem] * 2)(mine, swapped)
    pair, *back = lax.optimization_barrier((pair, *back))
    summed = lax.psum_scatter(
        pair.reshape(lat // 2, width), "dp", scatter_dimension=0, tiled=True,
        axis_index_groups=[list(range(c, replicas, 2)) for c in range(2)],
    )
    home = lax.cond(
        core[0] < 2,
        lambda stay, right, left: exchange(stay, right, left),
        lambda stay, right, left: jnp.concatenate([stay, right, left], axis=0),
        *back,
    )
    pick, weight = call(
        mask_kernel, [((rows, tokens), BF16), ((rows, tokens), F32)], specs=[smem] + [vmem] * 2
    )(plane, ids, probs)
    mixed, latent_gradient, gate_grad = call(
        combine_kernel,
        [((tokens, lat), BF16), ((tokens, lat), BF16), ((top, tokens), F32)],
        specs=[smem] + [vmem] * 5,
    )(plane, ids, pick, weight, cotangent, home)
    summed, mixed, latent_gradient, gate_grad = lax.optimization_barrier(
        (summed, mixed, latent_gradient, gate_grad)
    )
    gate_up_grad, down_grad = call(
        split_kernel,
        [((share, 2 * ffw), BF16), ((share, ffw), BF16)],
        scratch=[pltpu.SemaphoreType.DMA((2,))],
        specs=[pl.BlockSpec(memory_space=pl.ANY)],
        vmem=ALL_VMEM_BYTES,
    )(summed)
    return (mixed, latent_gradient, gate_grad.T, gate_up_grad[None], down_grad[None])


def exchange(stay, right, left):
    part, wide = stay.shape
    columns = lax.axis_size("expert")
    places = columns // RING
    up = [(e, (e + places) % columns) for e in range(columns)]
    down = [(e, (e - places) % columns) for e in range(columns)]
    half = part // 2
    one_right = lax.ppermute(right, "expert", up)
    one_left = lax.ppermute(left, "expert", down)
    two_right = lax.ppermute(one_right[part:], "expert", up)
    two_left = lax.ppermute(one_left[:half], "expert", down)
    pieces = [stay, one_right[:part], one_left[half:], jnp.concatenate([two_right, two_left], axis=0)]
    merged = jnp.concatenate([piece.reshape(places, GROUP, wide) for piece in pieces], axis=1)
    moved = lax.all_to_all(
        merged, "expert", split_axis=0, concat_axis=0, tiled=True,
        axis_index_groups=[list(range(z * places, (z + 1) * places)) for z in range(RING)],
    )
    return moved.reshape(RING * part, wide)


def solution(mesh):
    return jax.shard_map(
        local,
        mesh=mesh,
        in_specs=(
            P(("dp", "expert"), None),
            P(("dp", "expert"), None),
            P(("dp", "expert"), None),
            P(("dp", "expert"), None),
            P("expert", None, None),
            P("expert", None, None),
        ),
        out_specs=(
            P(("dp", "expert"), None),
            P(("dp", "expert"), None),
            P(("dp", "expert"), None),
            P("expert", "dp", None),
            P("expert", "dp", None),
        ),
        check_vma=False,
    )
```

```python
import jax
import jax.numpy as jnp
from jax import lax
from jax.experimental import pallas as pl
from jax.experimental.pallas import tpu as pltpu
from jax.sharding import PartitionSpec as P

EXP_DEV = 4
CAP = 2
GROUP = 4 * CAP
RING = 4
F32 = jnp.float32
BF16 = jnp.bfloat16
VMEM_BYTES = 48 << 20
ALL_VMEM_BYTES = 63 << 20


def mm(a, b, ca=1, cb=0):
    return lax.dot_general(a, b, (((ca,), (cb,)), ((), ())), preferred_element_type=F32)


def iota(shape, dim):
    return lax.broadcasted_iota(jnp.int32, shape, dim)


def halves(value):
    high = value.astype(BF16)
    return high, (value - high.astype(F32)).astype(BF16)


def leaving(row, rows):
    part = rows // RING
    return row // part, (row % part) // GROUP


def arriving(row):
    piece = (row // GROUP) % RING
    step = jnp.where(piece == 0, 0, jnp.where(piece == 1, RING - 1, piece - 1))
    return step, row // (GROUP * RING)


def block_index(step, place, plane, rows):
    return ((plane + step) % RING) * (rows // (GROUP * RING)) + place


def routing(ids_ref, probs_ref, expert):
    rows, tokens = expert.shape
    row = iota((rows, tokens), 0)
    named = jnp.zeros((rows, tokens), F32)
    gate = jnp.zeros((rows, tokens), F32)
    for slot in range(ids_ref.shape[0]):
        hit = ids_ref[slot : slot + 1, :] == expert
        named = jnp.where(hit, 1.0, named)
        gate = jnp.where(hit, probs_ref[slot : slot + 1, :], gate)
    before = iota((tokens, tokens), 0)
    after = iota((tokens, tokens), 1)
    earlier = mm(named.astype(BF16), jnp.where(before < after, 1.0, 0.0).astype(BF16))
    pick = (named > 0.5) & (earlier == (row & 1).astype(F32))
    kind = (row & 2) == 0
    half = (row & 4) == 0
    return pick, gate, kind, half


def zero_one(mask):
    return jnp.where(mask, 1.0, 0.0).astype(BF16)


def store_leaving(message, stay_ref, right_ref, left_ref):
    part = stay_ref.shape[0]
    middle = 2 * part + part // 2
    stay_ref[...] = message[:part]
    right_ref[...] = message[part:middle]
    left_ref[...] = message[middle:]


def pack_kernel(ids_hbm, probs_hbm, latent_hbm, cot_hbm, sent_ref, ids_ref, probs_ref, latent_ref, cot_ref, sems):
    rows, wide = sent_ref.shape
    pairs = [(ids_hbm, ids_ref), (probs_hbm, probs_ref), (latent_hbm, latent_ref), (cot_hbm, cot_ref)]
    copies = [pltpu.make_async_copy(a, b, sems.at[i]) for i, (a, b) in enumerate(pairs)]
    for copy in copies:
        copy.start()
    copies[0].wait()
    copies[1].wait()
    expert = iota((rows, ids_ref.shape[1]), 0) // GROUP * EXP_DEV
    pick, gate, first, low = routing(ids_ref, probs_ref, expert)
    token = jnp.where(pick & first, 1.0, 0.0)
    weight = jnp.where(pick & ~first, gate, 0.0)
    copies[2].wait()
    copies[3].wait()
    total = jnp.zeros((rows, wide), F32)
    for h in range(2):
        here = low if h == 0 else ~low
        high, rest = halves(jnp.where(here, weight, 0.0))
        picks = jnp.concatenate([jnp.where(here, token, 0.0).astype(BF16), high, rest], axis=1)
        cols = pl.ds(h * wide, wide)
        cot = cot_ref[:, cols]
        total = total + mm(picks, jnp.concatenate([latent_ref[:, cols], cot, cot], axis=0))
    sent_ref[...] = total.astype(BF16)


def sorted_position(index, slots):
    group = index // GROUP
    return ((index & 2) + ((index >> 2) & 1)) * slots + group * CAP + (index & 1)


def expert_kernel(
    core_ref, there_ref, win_ref, wout_ref, mine_ref, other_ref, act_ref, grad_ref, terms_ref
):
    rows, wide = there_ref.shape
    slots = rows // 4
    ffw = wout_ref.shape[1]
    share = mine_ref.shape[1]
    sort = zero_one(iota((rows, rows), 0) == sorted_position(iota((rows, rows), 1), slots))
    data = mm(sort, there_ref[...]).astype(BF16)
    vec = [data[:slots], data[slots : 2 * slots]]
    cot = [data[2 * slots : 3 * slots], data[3 * slots :]]
    top = [pl.ds(0, wide), pl.ds(wide, wide)]

    hidden = mm(vec[0], win_ref[top[0], :]) + mm(vec[1], win_ref[top[1], :])
    g = hidden[:, :ffw]
    u = hidden[:, ffw:]
    s = 1.0 / (1.0 + jnp.exp(-g))
    act = (g * s * u).astype(BF16)
    grad_act = mm(cot[0], wout_ref[top[0], :]) + mm(cot[1], wout_ref[top[1], :])
    grad_hidden = jnp.concatenate(
        [grad_act * u * s * (1.0 + g * (1.0 - s)), grad_act * g * s], axis=1
    ).astype(BF16)
    act_ref[...] = act
    grad_ref[...] = grad_hidden

    for h in range(2):
        terms_ref[top[h], : 2 * ffw] = mm(vec[h], grad_hidden, 0, 0).astype(BF16)
        terms_ref[top[h], 2 * ffw :] = mm(cot[h], act, 0, 0).astype(BF16)
    even = core_ref[0] == 0
    for block in range(mine_ref.shape[0]):
        a = terms_ref[pl.ds(2 * block * share, share), :]
        b = terms_ref[pl.ds((2 * block + 1) * share, share), :]
        mine_ref[block] = jnp.where(even, a, b)
        other_ref[block] = jnp.where(even, b, a)


def return_kernel(plane_ref, act_ref, grad_ref, win_ref, wout_ref, stay_ref, right_ref, left_ref):
    part, wide = stay_ref.shape
    rows = RING * part
    slots = rows // 4
    top = [pl.ds(0, wide), pl.ds(wide, wide)]
    act = act_ref[...]
    grad_hidden = grad_ref[...]
    result = jnp.concatenate(
        [mm(act, wout_ref[top[h], :], 1, 1).astype(BF16) for h in range(2)]
        + [mm(grad_hidden, win_ref[top[h], :], 1, 1).astype(BF16) for h in range(2)],
        axis=0,
    )
    row = iota((rows, rows), 0)
    step, place = leaving(row, rows)
    source = block_index(step, place, plane_ref[0], rows) * GROUP + row % GROUP
    unsort = zero_one(iota((rows, rows), 1) == sorted_position(source, slots))
    store_leaving(mm(unsort, result).astype(BF16), stay_ref, right_ref, left_ref)


def split_kernel(sum_hbm, gate_up_ref, down_ref, sems):
    cut = gate_up_ref.shape[1]
    copies = [
        pltpu.make_async_copy(sum_hbm.at[:, pl.ds(0, cut)], gate_up_ref, sems.at[0]),
        pltpu.make_async_copy(sum_hbm.at[:, pl.ds(cut, down_ref.shape[1])], down_ref, sems.at[1]),
    ]
    for copy in copies:
        copy.start()
    for copy in copies:
        copy.wait()


def add_kernel(a_ref, b_ref, out_ref):
    out_ref[...] = (a_ref[...].astype(F32) + b_ref[...].astype(F32)).astype(BF16)


def mask_kernel(plane_ref, ids_ref, probs_ref, pick_ref, weight_ref):
    step, place = arriving(iota(weight_ref.shape, 0))
    expert = block_index(step, place, plane_ref[0], weight_ref.shape[0]) * EXP_DEV
    pick, gate, first, _ = routing(ids_ref, probs_ref, expert)
    pick_ref[...] = zero_one(pick)
    weight_ref[...] = jnp.where(pick & first, gate, 0.0)


def combine_kernel(plane_ref, ids_ref, pick_ref, weight_ref, cot_ref, home_ref, mixed_ref, latgrad_ref, gate_ref):
    rows, wide = home_ref.shape
    weight = weight_ref[...]
    pick = pick_ref[...].astype(F32)
    row = iota(weight.shape, 0)
    step, place = arriving(row)
    expert = block_index(step, place, plane_ref[0], rows) * EXP_DEV
    first = (row & 2) == 0
    low = (row & 4) == 0
    home = home_ref[...]
    chosen = jnp.where(first, pick, 0.0)
    token = pick - chosen
    inner = jnp.zeros(weight.shape, F32)
    for h in range(2):
        here = low if h == 0 else ~low
        cols = pl.ds(h * wide, wide)
        high, rest = halves(jnp.where(here, weight, 0.0))
        mixed_ref[:, cols] = (mm(high, home, 0, 0) + mm(rest, home, 0, 0)).astype(BF16)
        latgrad_ref[:, cols] = mm(jnp.where(here, token, 0.0).astype(BF16), home, 0, 0).astype(BF16)
        inner = jnp.where(here, mm(home, cot_ref[:, cols], 1, 1), inner)
    inner = jnp.where(chosen > 0.5, inner, 0.0)
    for slot in range(ids_ref.shape[0]):
        hit = ids_ref[slot : slot + 1, :] == expert
        gate_ref[slot : slot + 1, :] = jnp.sum(jnp.where(hit, inner, 0.0), axis=0, keepdims=True)


def call(kernel, outs, scratch=(), specs=None, vmem=VMEM_BYTES):
    shapes = [jax.ShapeDtypeStruct(shape, dtype) for shape, dtype in outs]
    return pl.pallas_call(
        kernel,
        out_shape=shapes,
        in_specs=specs,
        out_specs=[pl.BlockSpec(memory_space=pltpu.VMEM)] * len(shapes),
        scratch_shapes=list(scratch),
        compiler_params=pltpu.CompilerParams(vmem_limit_bytes=vmem),
        name=kernel.__name__,
    )


def local(latent, expert_ids, gate_probs, cotangent, w_gate_up, w_down):
    tokens, lat = latent.shape
    top = expert_ids.shape[1]
    columns = lax.axis_size("expert")
    replicas = lax.axis_size("dp")
    ffw = w_down.shape[2]
    rows = columns * GROUP
    wide = lat // 2
    width = 3 * ffw
    share = lat // replicas
    ids = expert_ids.T
    probs = gate_probs.T
    vmem = pl.BlockSpec(memory_space=pltpu.VMEM)

    smem = pl.BlockSpec(memory_space=pltpu.SMEM)
    plane = (lax.axis_index("expert") // (columns // RING)).astype(jnp.int32).reshape(1)
    part = rows // RING
    leave = [((part, wide), BF16), ((part + part // 2, wide), BF16), ((part + part // 2, wide), BF16)]

    (sent,) = call(
        pack_kernel,
        [((rows, wide), BF16)],
        scratch=[pltpu.VMEM(a.shape, a.dtype) for a in (ids, probs, latent, cotangent)]
        + [pltpu.SemaphoreType.DMA((4,))],
        specs=[pl.BlockSpec(memory_space=pl.ANY)] * 4,
        vmem=ALL_VMEM_BYTES,
    )(ids, probs, latent, cotangent)
    there = lax.all_to_all(
        sent.reshape(columns, GROUP, wide), "expert", split_axis=0, concat_axis=0, tiled=True
    ).reshape(rows, wide)

    core = (lax.axis_index("dp") % 2).astype(jnp.int32).reshape(1)
    half_terms = ((replicas // 2, share, width), BF16)
    slots = columns * CAP
    mine, other, act, grad_hidden = call(
        expert_kernel,
        [half_terms, half_terms, ((slots, ffw), BF16), ((slots, 2 * ffw), BF16)],
        scratch=[pltpu.VMEM((lat, width), BF16)],
        specs=[smem] + [vmem] * 3,
    )(core, there, w_gate_up[0], w_down[0])

    swapped = lax.ppermute(other, "dp", [(i, i ^ 1) for i in range(replicas)])
    back = call(return_kernel, leave, specs=[smem] + [vmem] * 4)(
        plane, act, grad_hidden, w_gate_up[0], w_down[0]
    )
    (pair,) = call(add_kernel, [half_terms], specs=[vmem] * 2)(mine, swapped)
    pair, *back = lax.optimization_barrier((pair, *back))
    summed = lax.psum_scatter(
        pair.reshape(lat // 2, width), "dp", scatter_dimension=0, tiled=True,
        axis_index_groups=[list(range(c, replicas, 2)) for c in range(2)],
    )
    home = lax.cond(
        core[0] < 2,
        lambda stay, right, left: exchange(stay, right, left),
        lambda stay, right, left: jnp.concatenate([stay, right, left], axis=0),
        *back,
    )
    pick, weight = call(
        mask_kernel, [((rows, tokens), BF16), ((rows, tokens), F32)], specs=[smem] + [vmem] * 2
    )(plane, ids, probs)
    mixed, latent_gradient, gate_grad = call(
        combine_kernel,
        [((tokens, lat), BF16), ((tokens, lat), BF16), ((top, tokens), F32)],
        specs=[smem] + [vmem] * 5,
    )(plane, ids, pick, weight, cotangent, home)
    summed, mixed, latent_gradient, gate_grad = lax.optimization_barrier(
        (summed, mixed, latent_gradient, gate_grad)
    )
    gate_up_grad, down_grad = call(
        split_kernel,
        [((share, 2 * ffw), BF16), ((share, ffw), BF16)],
        scratch=[pltpu.SemaphoreType.DMA((2,))],
        specs=[pl.BlockSpec(memory_space=pl.ANY)],
        vmem=ALL_VMEM_BYTES,
    )(summed)
    return (mixed, latent_gradient, gate_grad.T, gate_up_grad[None], down_grad[None])


def exchange(stay, right, left):
    part, wide = stay.shape
    columns = lax.axis_size("expert")
    places = columns // RING
    up = [(e, (e + places) % columns) for e in range(columns)]
    down = [(e, (e - places) % columns) for e in range(columns)]
    half = part // 2
    one_right = lax.ppermute(right, "expert", up)
    one_left = lax.ppermute(left, "expert", down)
    two_right = lax.ppermute(one_right[part:], "expert", up)
    two_left = lax.ppermute(one_left[:half], "expert", down)
    pieces = [stay, one_right[:part], one_left[half:], jnp.concatenate([two_right, two_left], axis=0)]
    merged = jnp.concatenate([piece.reshape(places, GROUP, wide) for piece in pieces], axis=1)
    moved = lax.all_to_all(
        merged, "expert", split_axis=0, concat_axis=0, tiled=True,
        axis_index_groups=[list(range(z * places, (z + 1) * places)) for z in range(RING)],
    )
    return moved.reshape(RING * part, wide)


def solution(mesh):
    return jax.shard_map(
        local,
        mesh=mesh,
        in_specs=(
            P(("dp", "expert"), None),
            P(("dp", "expert"), None),
            P(("dp", "expert"), None),
            P(("dp", "expert"), None),
            P("expert", None, None),
            P("expert", None, None),
        ),
        out_specs=(
            P(("dp", "expert"), None),
            P(("dp", "expert"), None),
            P(("dp", "expert"), None),
            P("expert", "dp", None),
            P("expert", "dp", None),
        ),
        check_vma=False,
    )
```

```python
import jax
import jax.numpy as jnp
from jax import lax
from jax.experimental import pallas as pl
from jax.experimental.pallas import tpu as pltpu
from jax.sharding import PartitionSpec as P

EXP_DEV = 4
CAP = 2
GROUP = 4 * CAP
F32 = jnp.float32
BF16 = jnp.bfloat16
VMEM_BYTES = 48 << 20
ALL_VMEM_BYTES = 63 << 20


def mm(a, b, ca=1, cb=0):
    return lax.dot_general(a, b, (((ca,), (cb,)), ((), ())), preferred_element_type=F32)


def iota(shape, dim):
    return lax.broadcasted_iota(jnp.int32, shape, dim)


def halves(value):
    high = value.astype(BF16)
    return high, (value - high.astype(F32)).astype(BF16)


def routing(ids_ref, probs_ref, rows):
    tokens = ids_ref.shape[1]
    row = iota((rows, tokens), 0)
    expert = (row // GROUP) * EXP_DEV
    named = jnp.zeros((rows, tokens), F32)
    gate = jnp.zeros((rows, tokens), F32)
    for slot in range(ids_ref.shape[0]):
        hit = ids_ref[slot : slot + 1, :] == expert
        named = jnp.where(hit, 1.0, named)
        gate = jnp.where(hit, probs_ref[slot : slot + 1, :], gate)
    before = iota((tokens, tokens), 0)
    after = iota((tokens, tokens), 1)
    earlier = mm(named.astype(BF16), jnp.where(before < after, 1.0, 0.0).astype(BF16))
    pick = (named > 0.5) & (earlier == (row & 1).astype(F32))
    kind = (row & 2) == 0
    half = (row & 4) == 0
    return pick, gate, kind, half, expert


def zero_one(mask):
    return jnp.where(mask, 1.0, 0.0).astype(BF16)


def pack_kernel(ids_hbm, probs_hbm, latent_hbm, cot_hbm, sent_ref, ids_ref, probs_ref, latent_ref, cot_ref, sems):
    rows, wide = sent_ref.shape
    pairs = [(ids_hbm, ids_ref), (probs_hbm, probs_ref), (latent_hbm, latent_ref), (cot_hbm, cot_ref)]
    copies = [pltpu.make_async_copy(a, b, sems.at[i]) for i, (a, b) in enumerate(pairs)]
    for copy in copies:
        copy.start()
    copies[0].wait()
    copies[1].wait()
    pick, gate, first, low, _ = routing(ids_ref, probs_ref, rows)
    token = jnp.where(pick & first, 1.0, 0.0)
    weight = jnp.where(pick & ~first, gate, 0.0)
    copies[2].wait()
    copies[3].wait()
    total = jnp.zeros((rows, wide), F32)
    for h in range(2):
        here = low if h == 0 else ~low
        high, rest = halves(jnp.where(here, weight, 0.0))
        picks = jnp.concatenate([jnp.where(here, token, 0.0).astype(BF16), high, rest], axis=1)
        cols = pl.ds(h * wide, wide)
        cot = cot_ref[:, cols]
        total = total + mm(picks, jnp.concatenate([latent_ref[:, cols], cot, cot], axis=0))
    sent_ref[...] = total.astype(BF16)


def sorted_position(index, slots):
    group = index // GROUP
    return ((index & 2) + ((index >> 2) & 1)) * slots + group * CAP + (index & 1)


def expert_kernel(
    core_ref, there_ref, win_ref, wout_ref, mine_ref, other_ref, act_ref, grad_ref, terms_ref
):
    rows, wide = there_ref.shape
    slots = rows // 4
    ffw = wout_ref.shape[1]
    share = mine_ref.shape[1]
    sort = zero_one(iota((rows, rows), 0) == sorted_position(iota((rows, rows), 1), slots))
    data = mm(sort, there_ref[...]).astype(BF16)
    vec = [data[:slots], data[slots : 2 * slots]]
    cot = [data[2 * slots : 3 * slots], data[3 * slots :]]
    top = [pl.ds(0, wide), pl.ds(wide, wide)]

    hidden = mm(vec[0], win_ref[top[0], :]) + mm(vec[1], win_ref[top[1], :])
    g = hidden[:, :ffw]
    u = hidden[:, ffw:]
    s = 1.0 / (1.0 + jnp.exp(-g))
    act = (g * s * u).astype(BF16)
    grad_act = mm(cot[0], wout_ref[top[0], :]) + mm(cot[1], wout_ref[top[1], :])
    grad_hidden = jnp.concatenate(
        [grad_act * u * s * (1.0 + g * (1.0 - s)), grad_act * g * s], axis=1
    ).astype(BF16)
    act_ref[...] = act
    grad_ref[...] = grad_hidden

    for h in range(2):
        terms_ref[top[h], : 2 * ffw] = mm(vec[h], grad_hidden, 0, 0).astype(BF16)
        terms_ref[top[h], 2 * ffw :] = mm(cot[h], act, 0, 0).astype(BF16)
    even = core_ref[0] == 0
    for block in range(mine_ref.shape[0]):
        a = terms_ref[pl.ds(2 * block * share, share), :]
        b = terms_ref[pl.ds((2 * block + 1) * share, share), :]
        mine_ref[block] = jnp.where(even, a, b)
        other_ref[block] = jnp.where(even, b, a)


def return_kernel(act_ref, grad_ref, win_ref, wout_ref, back_ref):
    rows, wide = back_ref.shape
    slots = rows // 4
    top = [pl.ds(0, wide), pl.ds(wide, wide)]
    act = act_ref[...]
    grad_hidden = grad_ref[...]
    result = jnp.concatenate(
        [mm(act, wout_ref[top[h], :], 1, 1).astype(BF16) for h in range(2)]
        + [mm(grad_hidden, win_ref[top[h], :], 1, 1).astype(BF16) for h in range(2)],
        axis=0,
    )
    unsort = zero_one(iota((rows, rows), 1) == sorted_position(iota((rows, rows), 0), slots))
    back_ref[...] = mm(unsort, result).astype(BF16)


def add_kernel(bit_ref, a_ref, b_ref, out_ref):
    bit = bit_ref[0]
    for block in range(out_ref.shape[0]):
        index = 2 * block + bit
        out_ref[block] = (a_ref[index].astype(F32) + b_ref[index].astype(F32)).astype(BF16)


def last_add_kernel(a_ref, b_ref, gate_up_ref, down_ref):
    cut = gate_up_ref.shape[1]
    total = (a_ref[0].astype(F32) + b_ref[0].astype(F32)).astype(BF16)
    gate_up_ref[...] = total[:, :cut]
    down_ref[...] = total[:, cut:]


def mask_kernel(ids_ref, probs_ref, pick_ref, weight_ref):
    pick, gate, first, _, _ = routing(ids_ref, probs_ref, weight_ref.shape[0])
    pick_ref[...] = zero_one(pick)
    weight_ref[...] = jnp.where(pick & first, gate, 0.0)


def combine_kernel(ids_ref, pick_ref, weight_ref, cot_ref, home_ref, mixed_ref, latgrad_ref, gate_ref):
    rows, wide = home_ref.shape
    weight = weight_ref[...]
    pick = pick_ref[...].astype(F32)
    row = iota(weight.shape, 0)
    expert = (row // GROUP) * EXP_DEV
    first = (row & 2) == 0
    low = (row & 4) == 0
    home = home_ref[...]
    chosen = jnp.where(first, pick, 0.0)
    token = pick - chosen
    inner = jnp.zeros(weight.shape, F32)
    for h in range(2):
        here = low if h == 0 else ~low
        cols = pl.ds(h * wide, wide)
        high, rest = halves(jnp.where(here, weight, 0.0))
        mixed_ref[:, cols] = (mm(high, home, 0, 0) + mm(rest, home, 0, 0)).astype(BF16)
        latgrad_ref[:, cols] = mm(jnp.where(here, token, 0.0).astype(BF16), home, 0, 0).astype(BF16)
        inner = jnp.where(here, mm(home, cot_ref[:, cols], 1, 1), inner)
    inner = jnp.where(chosen > 0.5, inner, 0.0)
    for slot in range(ids_ref.shape[0]):
        hit = ids_ref[slot : slot + 1, :] == expert
        gate_ref[slot : slot + 1, :] = jnp.sum(jnp.where(hit, inner, 0.0), axis=0, keepdims=True)


def call(kernel, outs, scratch=(), specs=None, vmem=VMEM_BYTES):
    shapes = [jax.ShapeDtypeStruct(shape, dtype) for shape, dtype in outs]
    return pl.pallas_call(
        kernel,
        out_shape=shapes,
        in_specs=specs,
        out_specs=[pl.BlockSpec(memory_space=pltpu.VMEM)] * len(shapes),
        scratch_shapes=list(scratch),
        compiler_params=pltpu.CompilerParams(vmem_limit_bytes=vmem),
        name=kernel.__name__,
    )


def local(latent, expert_ids, gate_probs, cotangent, w_gate_up, w_down):
    tokens, lat = latent.shape
    top = expert_ids.shape[1]
    columns = lax.axis_size("expert")
    replicas = lax.axis_size("dp")
    ffw = w_down.shape[2]
    rows = columns * GROUP
    wide = lat // 2
    width = 3 * ffw
    share = lat // replicas
    ids = expert_ids.T
    probs = gate_probs.T
    vmem = pl.BlockSpec(memory_space=pltpu.VMEM)
    smem = pl.BlockSpec(memory_space=pltpu.SMEM)

    (sent,) = call(
        pack_kernel,
        [((rows, wide), BF16)],
        scratch=[pltpu.VMEM(a.shape, a.dtype) for a in (ids, probs, latent, cotangent)]
        + [pltpu.SemaphoreType.DMA((4,))],
        specs=[pl.BlockSpec(memory_space=pl.ANY)] * 4,
        vmem=ALL_VMEM_BYTES,
    )(ids, probs, latent, cotangent)
    there = exchange(sent, columns)

    core = (lax.axis_index("dp") % 2).astype(jnp.int32).reshape(1)
    half_terms = ((replicas // 2, share, width), BF16)
    slots = columns * CAP
    mine, other, act, grad_hidden = call(
        expert_kernel,
        [half_terms, half_terms, ((slots, ffw), BF16), ((slots, 2 * ffw), BF16)],
        scratch=[pltpu.VMEM((lat, width), BF16)],
        specs=[smem] + [vmem] * 3,
    )(core, there, w_gate_up[0], w_down[0])

    position = lax.axis_index("dp") // 2
    chips = replicas // 2
    arrived = lax.ppermute(other, "dp", [(i, i ^ 1) for i in range(replicas)])
    kept = mine
    (back,) = call(return_kernel, [((rows, wide), BF16)], specs=[vmem] * 4)(
        act, grad_hidden, w_gate_up[0], w_down[0]
    )
    home = None
    distance = 1
    while distance < chips:
        blocks = ((chips // (2 * distance), share, width), BF16)
        bit = (position // distance % 2).astype(jnp.int32).reshape(1)
        (send,) = call(add_kernel, [blocks], specs=[smem] + [vmem] * 2)(1 - bit, kept, arrived)
        moving = lax.ppermute(send, "dp", [(i, i ^ (2 * distance)) for i in range(replicas)])
        kept, send = lax.optimization_barrier((kept, send))
        (kept,) = call(add_kernel, [blocks], specs=[smem] + [vmem] * 2)(bit, kept, arrived)
        arrived = moving
        if home is None:
            kept, back = lax.optimization_barrier((kept, back))
            home = exchange(back, columns)
        distance *= 2
    if home is None:
        home = exchange(back, columns)
    pick, weight = call(
        mask_kernel, [((rows, tokens), BF16), ((rows, tokens), F32)], specs=[vmem] * 2
    )(ids, probs)
    mixed, latent_gradient, gate_grad = call(
        combine_kernel,
        [((tokens, lat), BF16), ((tokens, lat), BF16), ((top, tokens), F32)],
        specs=[vmem] * 5,
    )(ids, pick, weight, cotangent, home)
    gate_up_grad, down_grad = call(
        last_add_kernel, [((share, 2 * ffw), BF16), ((share, ffw), BF16)], specs=[vmem] * 2
    )(kept, arrived)
    return (mixed, latent_gradient, gate_grad.T, gate_up_grad[None], down_grad[None])


def exchange(message, columns):
    rows, wide = message.shape
    moved = lax.all_to_all(
        message.reshape(columns, rows // columns, wide), "expert", split_axis=0, concat_axis=0, tiled=True
    )
    return moved.reshape(rows, wide)


def solution(mesh):
    return jax.shard_map(
        local,
        mesh=mesh,
        in_specs=(
            P(("dp", "expert"), None),
            P(("dp", "expert"), None),
            P(("dp", "expert"), None),
            P(("dp", "expert"), None),
            P("expert", None, None),
            P("expert", None, None),
        ),
        out_specs=(
            P(("dp", "expert"), None),
            P(("dp", "expert"), None),
            P(("dp", "expert"), None),
            P("expert", "dp", None),
            P("expert", "dp", None),
        ),
        check_vma=False,
    )
```

```python
import jax
import jax.numpy as jnp
from jax import lax
from jax.experimental import pallas as pl
from jax.experimental.pallas import tpu as pltpu
from jax.sharding import PartitionSpec as P

EXP_DEV = 4
CAP = 2
GROUP = 4 * CAP
RING = 4
F32 = jnp.float32
BF16 = jnp.bfloat16
VMEM_BYTES = 48 << 20
ALL_VMEM_BYTES = 63 << 20


def mm(a, b, ca=1, cb=0):
    return lax.dot_general(a, b, (((ca,), (cb,)), ((), ())), preferred_element_type=F32)


def iota(shape, dim):
    return lax.broadcasted_iota(jnp.int32, shape, dim)


def halves(value):
    high = value.astype(BF16)
    return high, (value - high.astype(F32)).astype(BF16)


def leaving(row, rows):
    part = rows // RING
    return row // part, (row % part) // GROUP


def arriving(row):
    piece = (row // GROUP) % RING
    step = jnp.where(piece == 0, 0, jnp.where(piece == 1, RING - 1, piece - 1))
    return step, row // (GROUP * RING)


def block_index(step, place, plane, rows):
    return ((plane + step) % RING) * (rows // (GROUP * RING)) + place


def routing(ids_ref, probs_ref, expert):
    rows, tokens = expert.shape
    row = iota((rows, tokens), 0)
    named = jnp.zeros((rows, tokens), F32)
    gate = jnp.zeros((rows, tokens), F32)
    for slot in range(ids_ref.shape[0]):
        hit = ids_ref[slot : slot + 1, :] == expert
        named = jnp.where(hit, 1.0, named)
        gate = jnp.where(hit, probs_ref[slot : slot + 1, :], gate)
    before = iota((tokens, tokens), 0)
    after = iota((tokens, tokens), 1)
    earlier = mm(named.astype(BF16), jnp.where(before < after, 1.0, 0.0).astype(BF16))
    pick = (named > 0.5) & (earlier == (row & 1).astype(F32))
    kind = (row & 2) == 0
    half = (row & 4) == 0
    return pick, gate, kind, half


def zero_one(mask):
    return jnp.where(mask, 1.0, 0.0).astype(BF16)


def store_leaving(message, stay_ref, right_ref, left_ref):
    part = stay_ref.shape[0]
    middle = 2 * part + part // 2
    stay_ref[...] = message[:part]
    right_ref[...] = message[part:middle]
    left_ref[...] = message[middle:]


def pack_kernel(ids_hbm, probs_hbm, latent_hbm, cot_hbm, sent_ref, ids_ref, probs_ref, latent_ref, cot_ref, sems):
    rows, wide = sent_ref.shape
    pairs = [(ids_hbm, ids_ref), (probs_hbm, probs_ref), (latent_hbm, latent_ref), (cot_hbm, cot_ref)]
    copies = [pltpu.make_async_copy(a, b, sems.at[i]) for i, (a, b) in enumerate(pairs)]
    for copy in copies:
        copy.start()
    copies[0].wait()
    copies[1].wait()
    expert = iota((rows, ids_ref.shape[1]), 0) // GROUP * EXP_DEV
    pick, gate, first, low = routing(ids_ref, probs_ref, expert)
    token = jnp.where(pick & first, 1.0, 0.0)
    weight = jnp.where(pick & ~first, gate, 0.0)
    copies[2].wait()
    copies[3].wait()
    total = jnp.zeros((rows, wide), F32)
    for h in range(2):
        here = low if h == 0 else ~low
        high, rest = halves(jnp.where(here, weight, 0.0))
        picks = jnp.concatenate([jnp.where(here, token, 0.0).astype(BF16), high, rest], axis=1)
        cols = pl.ds(h * wide, wide)
        cot = cot_ref[:, cols]
        total = total + mm(picks, jnp.concatenate([latent_ref[:, cols], cot, cot], axis=0))
    sent_ref[...] = total.astype(BF16)


def sorted_position(index, slots):
    group = index // GROUP
    return ((index & 2) + ((index >> 2) & 1)) * slots + group * CAP + (index & 1)


def expert_kernel(
    core_ref, there_ref, win_ref, wout_ref, mine_ref, other_ref, act_ref, grad_ref, terms_ref
):
    rows, wide = there_ref.shape
    slots = rows // 4
    ffw = wout_ref.shape[1]
    share = mine_ref.shape[1]
    sort = zero_one(iota((rows, rows), 0) == sorted_position(iota((rows, rows), 1), slots))
    data = mm(sort, there_ref[...]).astype(BF16)
    vec = [data[:slots], data[slots : 2 * slots]]
    cot = [data[2 * slots : 3 * slots], data[3 * slots :]]
    top = [pl.ds(0, wide), pl.ds(wide, wide)]

    hidden = mm(vec[0], win_ref[top[0], :]) + mm(vec[1], win_ref[top[1], :])
    g = hidden[:, :ffw]
    u = hidden[:, ffw:]
    s = 1.0 / (1.0 + jnp.exp(-g))
    act = (g * s * u).astype(BF16)
    grad_act = mm(cot[0], wout_ref[top[0], :]) + mm(cot[1], wout_ref[top[1], :])
    grad_hidden = jnp.concatenate(
        [grad_act * u * s * (1.0 + g * (1.0 - s)), grad_act * g * s], axis=1
    ).astype(BF16)
    act_ref[...] = act
    grad_ref[...] = grad_hidden

    for h in range(2):
        terms_ref[top[h], : 2 * ffw] = mm(vec[h], grad_hidden, 0, 0).astype(BF16)
        terms_ref[top[h], 2 * ffw :] = mm(cot[h], act, 0, 0).astype(BF16)
    even = core_ref[0] == 0
    for block in range(mine_ref.shape[0]):
        a = terms_ref[pl.ds(2 * block * share, share), :]
        b = terms_ref[pl.ds((2 * block + 1) * share, share), :]
        mine_ref[block] = jnp.where(even, a, b)
        other_ref[block] = jnp.where(even, b, a)


def return_kernel(plane_ref, act_ref, grad_ref, win_ref, wout_ref, stay_ref, right_ref, left_ref):
    part, wide = stay_ref.shape
    rows = RING * part
    slots = rows // 4
    top = [pl.ds(0, wide), pl.ds(wide, wide)]
    act = act_ref[...]
    grad_hidden = grad_ref[...]
    result = jnp.concatenate(
        [mm(act, wout_ref[top[h], :], 1, 1).astype(BF16) for h in range(2)]
        + [mm(grad_hidden, win_ref[top[h], :], 1, 1).astype(BF16) for h in range(2)],
        axis=0,
    )
    row = iota((rows, rows), 0)
    step, place = leaving(row, rows)
    source = block_index(step, place, plane_ref[0], rows) * GROUP + row % GROUP
    unsort = zero_one(iota((rows, rows), 1) == sorted_position(source, slots))
    store_leaving(mm(unsort, result).astype(BF16), stay_ref, right_ref, left_ref)


def add_kernel(bit_ref, a_ref, b_ref, out_ref):
    bit = bit_ref[0]
    for block in range(out_ref.shape[0]):
        index = 2 * block + bit
        out_ref[block] = (a_ref[index].astype(F32) + b_ref[index].astype(F32)).astype(BF16)


def last_add_kernel(a_ref, b_ref, gate_up_ref, down_ref):
    cut = gate_up_ref.shape[1]
    total = (a_ref[0].astype(F32) + b_ref[0].astype(F32)).astype(BF16)
    gate_up_ref[...] = total[:, :cut]
    down_ref[...] = total[:, cut:]


def mask_kernel(plane_ref, ids_ref, probs_ref, pick_ref, weight_ref):
    step, place = arriving(iota(weight_ref.shape, 0))
    expert = block_index(step, place, plane_ref[0], weight_ref.shape[0]) * EXP_DEV
    pick, gate, first, _ = routing(ids_ref, probs_ref, expert)
    pick_ref[...] = zero_one(pick)
    weight_ref[...] = jnp.where(pick & first, gate, 0.0)


def combine_kernel(plane_ref, ids_ref, pick_ref, weight_ref, cot_ref, home_ref, mixed_ref, latgrad_ref, gate_ref):
    rows, wide = home_ref.shape
    weight = weight_ref[...]
    pick = pick_ref[...].astype(F32)
    row = iota(weight.shape, 0)
    step, place = arriving(row)
    expert = block_index(step, place, plane_ref[0], rows) * EXP_DEV
    first = (row & 2) == 0
    low = (row & 4) == 0
    home = home_ref[...]
    chosen = jnp.where(first, pick, 0.0)
    token = pick - chosen
    inner = jnp.zeros(weight.shape, F32)
    for h in range(2):
        here = low if h == 0 else ~low
        cols = pl.ds(h * wide, wide)
        high, rest = halves(jnp.where(here, weight, 0.0))
        mixed_ref[:, cols] = (mm(high, home, 0, 0) + mm(rest, home, 0, 0)).astype(BF16)
        latgrad_ref[:, cols] = mm(jnp.where(here, token, 0.0).astype(BF16), home, 0, 0).astype(BF16)
        inner = jnp.where(here, mm(home, cot_ref[:, cols], 1, 1), inner)
    inner = jnp.where(chosen > 0.5, inner, 0.0)
    for slot in range(ids_ref.shape[0]):
        hit = ids_ref[slot : slot + 1, :] == expert
        gate_ref[slot : slot + 1, :] = jnp.sum(jnp.where(hit, inner, 0.0), axis=0, keepdims=True)


def call(kernel, outs, scratch=(), specs=None, vmem=VMEM_BYTES):
    shapes = [jax.ShapeDtypeStruct(shape, dtype) for shape, dtype in outs]
    return pl.pallas_call(
        kernel,
        out_shape=shapes,
        in_specs=specs,
        out_specs=[pl.BlockSpec(memory_space=pltpu.VMEM)] * len(shapes),
        scratch_shapes=list(scratch),
        compiler_params=pltpu.CompilerParams(vmem_limit_bytes=vmem),
        name=kernel.__name__,
    )


def local(latent, expert_ids, gate_probs, cotangent, w_gate_up, w_down):
    tokens, lat = latent.shape
    top = expert_ids.shape[1]
    columns = lax.axis_size("expert")
    replicas = lax.axis_size("dp")
    ffw = w_down.shape[2]
    rows = columns * GROUP
    wide = lat // 2
    width = 3 * ffw
    share = lat // replicas
    ids = expert_ids.T
    probs = gate_probs.T
    vmem = pl.BlockSpec(memory_space=pltpu.VMEM)

    smem = pl.BlockSpec(memory_space=pltpu.SMEM)
    plane = (lax.axis_index("expert") // (columns // RING)).astype(jnp.int32).reshape(1)
    part = rows // RING
    leave = [((part, wide), BF16), ((part + part // 2, wide), BF16), ((part + part // 2, wide), BF16)]

    (sent,) = call(
        pack_kernel,
        [((rows, wide), BF16)],
        scratch=[pltpu.VMEM(a.shape, a.dtype) for a in (ids, probs, latent, cotangent)]
        + [pltpu.SemaphoreType.DMA((4,))],
        specs=[pl.BlockSpec(memory_space=pl.ANY)] * 4,
        vmem=ALL_VMEM_BYTES,
    )(ids, probs, latent, cotangent)
    there = lax.all_to_all(
        sent.reshape(columns, GROUP, wide), "expert", split_axis=0, concat_axis=0, tiled=True
    ).reshape(rows, wide)

    core = (lax.axis_index("dp") % 2).astype(jnp.int32).reshape(1)
    half_terms = ((replicas // 2, share, width), BF16)
    slots = columns * CAP
    mine, other, act, grad_hidden = call(
        expert_kernel,
        [half_terms, half_terms, ((slots, ffw), BF16), ((slots, 2 * ffw), BF16)],
        scratch=[pltpu.VMEM((lat, width), BF16)],
        specs=[smem] + [vmem] * 3,
    )(core, there, w_gate_up[0], w_down[0])

    position = lax.axis_index("dp") // 2
    chips = replicas // 2
    arrived = lax.ppermute(other, "dp", [(i, i ^ 1) for i in range(replicas)])
    kept = mine
    back = call(return_kernel, leave, specs=[smem] + [vmem] * 4)(
        plane, act, grad_hidden, w_gate_up[0], w_down[0]
    )
    steps = exchange(*back)
    carried = next(steps)
    distance = 1
    while distance < chips:
        blocks = ((chips // (2 * distance), share, width), BF16)
        bit = (position // distance % 2).astype(jnp.int32).reshape(1)
        (send,) = call(add_kernel, [blocks], specs=[smem] + [vmem] * 2)(1 - bit, kept, arrived)
        moving = lax.ppermute(send, "dp", [(i, i ^ (2 * distance)) for i in range(replicas)])
        kept, send = lax.optimization_barrier((kept, send))
        (kept,) = call(add_kernel, [blocks], specs=[smem] + [vmem] * 2)(bit, kept, arrived)
        arrived = moving
        distance *= 2
        if carried is not None and distance < chips:
            arrived, carried = lax.optimization_barrier((arrived, carried))
            home, carried = carried, steps.send(carried)
    while carried is not None:
        home, carried = carried, steps.send(carried)
    pick, weight = call(
        mask_kernel, [((rows, tokens), BF16), ((rows, tokens), F32)], specs=[smem] + [vmem] * 2
    )(plane, ids, probs)
    mixed, latent_gradient, gate_grad = call(
        combine_kernel,
        [((tokens, lat), BF16), ((tokens, lat), BF16), ((top, tokens), F32)],
        specs=[smem] + [vmem] * 5,
    )(plane, ids, pick, weight, cotangent, home)
    gate_up_grad, down_grad = call(
        last_add_kernel, [((share, 2 * ffw), BF16), ((share, ffw), BF16)], specs=[vmem] * 2
    )(kept, arrived)
    return (mixed, latent_gradient, gate_grad.T, gate_up_grad[None], down_grad[None])


def exchange(stay, right, left):
    part, wide = stay.shape
    columns = lax.axis_size("expert")
    places = columns // RING
    up = [(e, (e + places) % columns) for e in range(columns)]
    down = [(e, (e - places) % columns) for e in range(columns)]
    half = part // 2
    one_right, one_left = yield lax.ppermute(right, "expert", up), lax.ppermute(left, "expert", down)
    two_right, two_left = yield (
        lax.ppermute(one_right[part:], "expert", up), lax.ppermute(one_left[:half], "expert", down)
    )
    pieces = [stay, one_right[:part], one_left[half:], jnp.concatenate([two_right, two_left], axis=0)]
    merged = jnp.concatenate([piece.reshape(places, GROUP, wide) for piece in pieces], axis=1)
    moved = lax.all_to_all(
        merged, "expert", split_axis=0, concat_axis=0, tiled=True,
        axis_index_groups=[list(range(z * places, (z + 1) * places)) for z in range(RING)],
    )
    yield moved.reshape(RING * part, wide)
    yield None


def solution(mesh):
    return jax.shard_map(
        local,
        mesh=mesh,
        in_specs=(
            P(("dp", "expert"), None),
            P(("dp", "expert"), None),
            P(("dp", "expert"), None),
            P(("dp", "expert"), None),
            P("expert", None, None),
            P("expert", None, None),
        ),
        out_specs=(
            P(("dp", "expert"), None),
            P(("dp", "expert"), None),
            P(("dp", "expert"), None),
            P("expert", "dp", None),
            P("expert", "dp", None),
        ),
        check_vma=False,
    )
```

```python
import jax
import jax.numpy as jnp
from jax import lax
from jax.experimental import pallas as pl
from jax.experimental.pallas import tpu as pltpu
from jax.sharding import PartitionSpec as P

EXP_DEV = 4
CAP = 2
GROUP = 4 * CAP
F32 = jnp.float32
BF16 = jnp.bfloat16
VMEM_BYTES = 48 << 20
ALL_VMEM_BYTES = 63 << 20


def mm(a, b, ca=1, cb=0):
    return lax.dot_general(a, b, (((ca,), (cb,)), ((), ())), preferred_element_type=F32)


def iota(shape, dim):
    return lax.broadcasted_iota(jnp.int32, shape, dim)


def halves(value):
    high = value.astype(BF16)
    return high, (value - high.astype(F32)).astype(BF16)


def routing(ids_ref, probs_ref, rows):
    tokens = ids_ref.shape[1]
    row = iota((rows, tokens), 0)
    expert = (row // GROUP) * EXP_DEV
    named = jnp.zeros((rows, tokens), F32)
    gate = jnp.zeros((rows, tokens), F32)
    for slot in range(ids_ref.shape[0]):
        hit = ids_ref[slot : slot + 1, :] == expert
        named = jnp.where(hit, 1.0, named)
        gate = jnp.where(hit, probs_ref[slot : slot + 1, :], gate)
    before = iota((tokens, tokens), 0)
    after = iota((tokens, tokens), 1)
    earlier = mm(named.astype(BF16), jnp.where(before < after, 1.0, 0.0).astype(BF16))
    pick = (named > 0.5) & (earlier == (row & 1).astype(F32))
    kind = (row & 2) == 0
    half = (row & 4) == 0
    return pick, gate, kind, half, expert


def zero_one(mask):
    return jnp.where(mask, 1.0, 0.0).astype(BF16)


def pack_kernel(ids_hbm, probs_hbm, latent_hbm, cot_hbm, sent_ref, ids_ref, probs_ref, latent_ref, cot_ref, sems):
    rows, wide = sent_ref.shape
    pairs = [(ids_hbm, ids_ref), (probs_hbm, probs_ref), (latent_hbm, latent_ref), (cot_hbm, cot_ref)]
    copies = [pltpu.make_async_copy(a, b, sems.at[i]) for i, (a, b) in enumerate(pairs)]
    for copy in copies:
        copy.start()
    copies[0].wait()
    copies[1].wait()
    pick, gate, first, low, _ = routing(ids_ref, probs_ref, rows)
    token = jnp.where(pick & first, 1.0, 0.0)
    weight = jnp.where(pick & ~first, gate, 0.0)
    copies[2].wait()
    copies[3].wait()
    total = jnp.zeros((rows, wide), F32)
    for h in range(2):
        here = low if h == 0 else ~low
        high, rest = halves(jnp.where(here, weight, 0.0))
        picks = jnp.concatenate([jnp.where(here, token, 0.0).astype(BF16), high, rest], axis=1)
        cols = pl.ds(h * wide, wide)
        cot = cot_ref[:, cols]
        total = total + mm(picks, jnp.concatenate([latent_ref[:, cols], cot, cot], axis=0))
    sent_ref[...] = total.astype(BF16)


def sorted_position(index, slots):
    group = index // GROUP
    return ((index & 2) + ((index >> 2) & 1)) * slots + group * CAP + (index & 1)


def expert_kernel(
    core_ref, there_ref, win_ref, wout_ref, mine_ref, other_ref, act_ref, grad_ref, terms_ref
):
    rows, wide = there_ref.shape
    slots = rows // 4
    ffw = wout_ref.shape[1]
    share = mine_ref.shape[1]
    sort = zero_one(iota((rows, rows), 0) == sorted_position(iota((rows, rows), 1), slots))
    data = mm(sort, there_ref[...]).astype(BF16)
    vec = [data[:slots], data[slots : 2 * slots]]
    cot = [data[2 * slots : 3 * slots], data[3 * slots :]]
    top = [pl.ds(0, wide), pl.ds(wide, wide)]

    hidden = mm(vec[0], win_ref[top[0], :]) + mm(vec[1], win_ref[top[1], :])
    g = hidden[:, :ffw]
    u = hidden[:, ffw:]
    s = 1.0 / (1.0 + jnp.exp(-g))
    act = (g * s * u).astype(BF16)
    grad_act = mm(cot[0], wout_ref[top[0], :]) + mm(cot[1], wout_ref[top[1], :])
    grad_hidden = jnp.concatenate(
        [grad_act * u * s * (1.0 + g * (1.0 - s)), grad_act * g * s], axis=1
    ).astype(BF16)
    act_ref[...] = act
    grad_ref[...] = grad_hidden

    for h in range(2):
        terms_ref[top[h], : 2 * ffw] = mm(vec[h], grad_hidden, 0, 0).astype(BF16)
        terms_ref[top[h], 2 * ffw :] = mm(cot[h], act, 0, 0).astype(BF16)
    even = core_ref[0] == 0
    for block in range(mine_ref.shape[0]):
        a = terms_ref[pl.ds(2 * block * share, share), :]
        b = terms_ref[pl.ds((2 * block + 1) * share, share), :]
        mine_ref[block] = jnp.where(even, a, b)
        other_ref[block] = jnp.where(even, b, a)


def return_kernel(act_ref, grad_ref, win_ref, wout_ref, back_ref):
    rows, wide = back_ref.shape
    slots = rows // 4
    top = [pl.ds(0, wide), pl.ds(wide, wide)]
    act = act_ref[...]
    grad_hidden = grad_ref[...]
    result = jnp.concatenate(
        [mm(act, wout_ref[top[h], :], 1, 1).astype(BF16) for h in range(2)]
        + [mm(grad_hidden, win_ref[top[h], :], 1, 1).astype(BF16) for h in range(2)],
        axis=0,
    )
    unsort = zero_one(iota((rows, rows), 1) == sorted_position(iota((rows, rows), 0), slots))
    back_ref[...] = mm(unsort, result).astype(BF16)


def add_kernel(bit_ref, a_ref, b_ref, out_ref):
    bit = bit_ref[0]
    for block in range(out_ref.shape[0]):
        index = 2 * block + bit
        out_ref[block] = (a_ref[index].astype(F32) + b_ref[index].astype(F32)).astype(BF16)


def spread_kernel(place_ref, a_ref, b_ref, *out_refs):
    for step, out_ref in enumerate(out_refs):
        index = place_ref[step]
        out_ref[...] = (a_ref[index].astype(F32) + b_ref[index].astype(F32)).astype(BF16)


def last_add_kernel(*refs):
    *term_refs, gate_up_ref, down_ref = refs
    cut = gate_up_ref.shape[1]
    total = term_refs[0][...].astype(F32)
    for ref in term_refs[1:]:
        total = total + ref[...].astype(F32)
    gate_up_ref[...] = total[:, :cut].astype(BF16)
    down_ref[...] = total[:, cut:].astype(BF16)


def mask_kernel(ids_ref, probs_ref, pick_ref, weight_ref):
    pick, gate, first, _, _ = routing(ids_ref, probs_ref, weight_ref.shape[0])
    pick_ref[...] = zero_one(pick)
    weight_ref[...] = jnp.where(pick & first, gate, 0.0)


def combine_kernel(ids_ref, pick_ref, weight_ref, cot_ref, home_ref, mixed_ref, latgrad_ref, gate_ref):
    rows, wide = home_ref.shape
    weight = weight_ref[...]
    pick = pick_ref[...].astype(F32)
    row = iota(weight.shape, 0)
    expert = (row // GROUP) * EXP_DEV
    first = (row & 2) == 0
    low = (row & 4) == 0
    home = home_ref[...]
    chosen = jnp.where(first, pick, 0.0)
    token = pick - chosen
    inner = jnp.zeros(weight.shape, F32)
    for h in range(2):
        here = low if h == 0 else ~low
        cols = pl.ds(h * wide, wide)
        high, rest = halves(jnp.where(here, weight, 0.0))
        mixed_ref[:, cols] = (mm(high, home, 0, 0) + mm(rest, home, 0, 0)).astype(BF16)
        latgrad_ref[:, cols] = mm(jnp.where(here, token, 0.0).astype(BF16), home, 0, 0).astype(BF16)
        inner = jnp.where(here, mm(home, cot_ref[:, cols], 1, 1), inner)
    inner = jnp.where(chosen > 0.5, inner, 0.0)
    for slot in range(ids_ref.shape[0]):
        hit = ids_ref[slot : slot + 1, :] == expert
        gate_ref[slot : slot + 1, :] = jnp.sum(jnp.where(hit, inner, 0.0), axis=0, keepdims=True)


def call(kernel, outs, scratch=(), specs=None, vmem=VMEM_BYTES):
    shapes = [jax.ShapeDtypeStruct(shape, dtype) for shape, dtype in outs]
    return pl.pallas_call(
        kernel,
        out_shape=shapes,
        in_specs=specs,
        out_specs=[pl.BlockSpec(memory_space=pltpu.VMEM)] * len(shapes),
        scratch_shapes=list(scratch),
        compiler_params=pltpu.CompilerParams(vmem_limit_bytes=vmem),
        name=kernel.__name__,
    )


def local(latent, expert_ids, gate_probs, cotangent, w_gate_up, w_down):
    tokens, lat = latent.shape
    top = expert_ids.shape[1]
    columns = lax.axis_size("expert")
    replicas = lax.axis_size("dp")
    ffw = w_down.shape[2]
    rows = columns * GROUP
    wide = lat // 2
    width = 3 * ffw
    share = lat // replicas
    ids = expert_ids.T
    probs = gate_probs.T
    vmem = pl.BlockSpec(memory_space=pltpu.VMEM)
    smem = pl.BlockSpec(memory_space=pltpu.SMEM)

    (sent,) = call(
        pack_kernel,
        [((rows, wide), BF16)],
        scratch=[pltpu.VMEM(a.shape, a.dtype) for a in (ids, probs, latent, cotangent)]
        + [pltpu.SemaphoreType.DMA((4,))],
        specs=[pl.BlockSpec(memory_space=pl.ANY)] * 4,
        vmem=ALL_VMEM_BYTES,
    )(ids, probs, latent, cotangent)
    there = exchange(sent, columns)

    core = (lax.axis_index("dp") % 2).astype(jnp.int32).reshape(1)
    half_terms = ((replicas // 2, share, width), BF16)
    slots = columns * CAP
    mine, other, act, grad_hidden = call(
        expert_kernel,
        [half_terms, half_terms, ((slots, ffw), BF16), ((slots, 2 * ffw), BF16)],
        scratch=[pltpu.VMEM((lat, width), BF16)],
        specs=[smem] + [vmem] * 3,
    )(core, there, w_gate_up[0], w_down[0])

    position = lax.axis_index("dp") // 2
    chips = replicas // 2
    arrived = lax.ppermute(other, "dp", [(i, i ^ 1) for i in range(replicas)])
    kept = mine
    (back,) = call(return_kernel, [((rows, wide), BF16)], specs=[vmem] * 4)(
        act, grad_hidden, w_gate_up[0], w_down[0]
    )
    half_blocks = ((chips // 2, share, width), BF16)
    bit = (position % 2).astype(jnp.int32).reshape(1)
    (send,) = call(add_kernel, [half_blocks], specs=[smem] + [vmem] * 2)(1 - bit, kept, arrived)
    moving = lax.ppermute(send, "dp", [(i, i ^ 2) for i in range(replicas)])
    kept, send = lax.optimization_barrier((kept, send))
    (kept,) = call(add_kernel, [half_blocks], specs=[smem] + [vmem] * 2)(bit, kept, arrived)
    kept, back = lax.optimization_barrier((kept, back))
    home = lax.cond(core[0] < 2, lambda b: exchange(b, columns), lambda b: b, back)
    pick, weight = call(
        mask_kernel, [((rows, tokens), BF16), ((rows, tokens), F32)], specs=[vmem] * 2
    )(ids, probs)
    block = ((share, width), BF16)
    places = ((position // 2) ^ jnp.arange(chips // 2)).astype(jnp.int32)
    moving, home = lax.optimization_barrier((moving, home))
    terms = call(spread_kernel, [block] * (chips // 2), specs=[smem] + [vmem] * 2)(places, kept, moving)
    arrivals = [
        lax.ppermute(terms[step], "dp", [(i, i ^ (4 * step)) for i in range(replicas)])
        for step in range(1, chips // 2)
    ]
    gate_up_grad, down_grad = call(
        last_add_kernel, [((share, 2 * ffw), BF16), ((share, ffw), BF16)], specs=[vmem] * (chips // 2)
    )(terms[0], *arrivals)
    mixed, latent_gradient, gate_grad = call(
        combine_kernel,
        [((tokens, lat), BF16), ((tokens, lat), BF16), ((top, tokens), F32)],
        specs=[vmem] * 5,
    )(ids, pick, weight, cotangent, home)
    return (mixed, latent_gradient, gate_grad.T, gate_up_grad[None], down_grad[None])


def exchange(message, columns):
    rows, wide = message.shape
    moved = lax.all_to_all(
        message.reshape(columns, rows // columns, wide), "expert", split_axis=0, concat_axis=0, tiled=True
    )
    return moved.reshape(rows, wide)


def solution(mesh):
    return jax.shard_map(
        local,
        mesh=mesh,
        in_specs=(
            P(("dp", "expert"), None),
            P(("dp", "expert"), None),
            P(("dp", "expert"), None),
            P(("dp", "expert"), None),
            P("expert", None, None),
            P("expert", None, None),
        ),
        out_specs=(
            P(("dp", "expert"), None),
            P(("dp", "expert"), None),
            P(("dp", "expert"), None),
            P("expert", "dp", None),
            P("expert", "dp", None),
        ),
        check_vma=False,
    )
```

```python
import jax
import jax.numpy as jnp
from jax import lax
from jax.experimental import pallas as pl
from jax.experimental.pallas import tpu as pltpu
from jax.sharding import PartitionSpec as P

EXP_DEV = 4
CAP = 2
GROUP = 4 * CAP
RING = 4
F32 = jnp.float32
BF16 = jnp.bfloat16
VMEM_BYTES = 48 << 20
ALL_VMEM_BYTES = 63 << 20


def mm(a, b, ca=1, cb=0):
    return lax.dot_general(a, b, (((ca,), (cb,)), ((), ())), preferred_element_type=F32)


def iota(shape, dim):
    return lax.broadcasted_iota(jnp.int32, shape, dim)


def halves(value):
    high = value.astype(BF16)
    return high, (value - high.astype(F32)).astype(BF16)


def leaving(row, rows):
    part = rows // RING
    return row // part, (row % part) // GROUP


def arriving(row):
    piece = (row // GROUP) % RING
    step = jnp.where(piece == 0, 0, jnp.where(piece == 1, RING - 1, piece - 1))
    return step, row // (GROUP * RING)


def block_index(step, place, plane, rows):
    return ((plane + step) % RING) * (rows // (GROUP * RING)) + place


def routing(ids_ref, probs_ref, expert):
    rows, tokens = expert.shape
    row = iota((rows, tokens), 0)
    named = jnp.zeros((rows, tokens), F32)
    gate = jnp.zeros((rows, tokens), F32)
    for slot in range(ids_ref.shape[0]):
        hit = ids_ref[slot : slot + 1, :] == expert
        named = jnp.where(hit, 1.0, named)
        gate = jnp.where(hit, probs_ref[slot : slot + 1, :], gate)
    before = iota((tokens, tokens), 0)
    after = iota((tokens, tokens), 1)
    earlier = mm(named.astype(BF16), jnp.where(before < after, 1.0, 0.0).astype(BF16))
    pick = (named > 0.5) & (earlier == (row & 1).astype(F32))
    kind = (row & 2) == 0
    half = (row & 4) == 0
    return pick, gate, kind, half


def zero_one(mask):
    return jnp.where(mask, 1.0, 0.0).astype(BF16)


def store_leaving(message, stay_ref, right_ref, left_ref):
    part = stay_ref.shape[0]
    middle = 2 * part + part // 2
    stay_ref[...] = message[:part]
    right_ref[...] = message[part:middle]
    left_ref[...] = message[middle:]


def pack_kernel(ids_hbm, probs_hbm, latent_hbm, cot_hbm, sent_ref, ids_ref, probs_ref, latent_ref, cot_ref, sems):
    rows, wide = sent_ref.shape
    pairs = [(ids_hbm, ids_ref), (probs_hbm, probs_ref), (latent_hbm, latent_ref), (cot_hbm, cot_ref)]
    copies = [pltpu.make_async_copy(a, b, sems.at[i]) for i, (a, b) in enumerate(pairs)]
    for copy in copies:
        copy.start()
    copies[0].wait()
    copies[1].wait()
    expert = iota((rows, ids_ref.shape[1]), 0) // GROUP * EXP_DEV
    pick, gate, first, low = routing(ids_ref, probs_ref, expert)
    token = jnp.where(pick & first, 1.0, 0.0)
    weight = jnp.where(pick & ~first, gate, 0.0)
    copies[2].wait()
    copies[3].wait()
    total = jnp.zeros((rows, wide), F32)
    for h in range(2):
        here = low if h == 0 else ~low
        high, rest = halves(jnp.where(here, weight, 0.0))
        picks = jnp.concatenate([jnp.where(here, token, 0.0).astype(BF16), high, rest], axis=1)
        cols = pl.ds(h * wide, wide)
        cot = cot_ref[:, cols]
        total = total + mm(picks, jnp.concatenate([latent_ref[:, cols], cot, cot], axis=0))
    sent_ref[...] = total.astype(BF16)


def sorted_position(index, slots):
    group = index // GROUP
    return ((index & 2) + ((index >> 2) & 1)) * slots + group * CAP + (index & 1)


def expert_kernel(
    core_ref, there_ref, win_ref, wout_ref, mine_ref, other_ref, act_ref, grad_ref, terms_ref
):
    rows, wide = there_ref.shape
    slots = rows // 4
    ffw = wout_ref.shape[1]
    share = mine_ref.shape[1]
    sort = zero_one(iota((rows, rows), 0) == sorted_position(iota((rows, rows), 1), slots))
    data = mm(sort, there_ref[...]).astype(BF16)
    vec = [data[:slots], data[slots : 2 * slots]]
    cot = [data[2 * slots : 3 * slots], data[3 * slots :]]
    top = [pl.ds(0, wide), pl.ds(wide, wide)]

    hidden = mm(vec[0], win_ref[top[0], :]) + mm(vec[1], win_ref[top[1], :])
    g = hidden[:, :ffw]
    u = hidden[:, ffw:]
    s = 1.0 / (1.0 + jnp.exp(-g))
    act = (g * s * u).astype(BF16)
    grad_act = mm(cot[0], wout_ref[top[0], :]) + mm(cot[1], wout_ref[top[1], :])
    grad_hidden = jnp.concatenate(
        [grad_act * u * s * (1.0 + g * (1.0 - s)), grad_act * g * s], axis=1
    ).astype(BF16)
    act_ref[...] = act
    grad_ref[...] = grad_hidden

    for h in range(2):
        terms_ref[top[h], : 2 * ffw] = mm(vec[h], grad_hidden, 0, 0).astype(BF16)
        terms_ref[top[h], 2 * ffw :] = mm(cot[h], act, 0, 0).astype(BF16)
    even = core_ref[0] == 0
    for block in range(mine_ref.shape[0]):
        a = terms_ref[pl.ds(2 * block * share, share), :]
        b = terms_ref[pl.ds((2 * block + 1) * share, share), :]
        mine_ref[block] = jnp.where(even, a, b)
        other_ref[block] = jnp.where(even, b, a)


def return_kernel(plane_ref, act_ref, grad_ref, win_ref, wout_ref, stay_ref, right_ref, left_ref):
    part, wide = stay_ref.shape
    rows = RING * part
    slots = rows // 4
    top = [pl.ds(0, wide), pl.ds(wide, wide)]
    act = act_ref[...]
    grad_hidden = grad_ref[...]
    result = jnp.concatenate(
        [mm(act, wout_ref[top[h], :], 1, 1).astype(BF16) for h in range(2)]
        + [mm(grad_hidden, win_ref[top[h], :], 1, 1).astype(BF16) for h in range(2)],
        axis=0,
    )
    row = iota((rows, rows), 0)
    step, place = leaving(row, rows)
    source = block_index(step, place, plane_ref[0], rows) * GROUP + row % GROUP
    unsort = zero_one(iota((rows, rows), 1) == sorted_position(source, slots))
    store_leaving(mm(unsort, result).astype(BF16), stay_ref, right_ref, left_ref)


def split_kernel(sum_hbm, gate_up_ref, down_ref, sems):
    cut = gate_up_ref.shape[1]
    copies = [
        pltpu.make_async_copy(sum_hbm.at[:, pl.ds(0, cut)], gate_up_ref, sems.at[0]),
        pltpu.make_async_copy(sum_hbm.at[:, pl.ds(cut, down_ref.shape[1])], down_ref, sems.at[1]),
    ]
    for copy in copies:
        copy.start()
    for copy in copies:
        copy.wait()


def add_kernel(a_ref, b_ref, out_ref):
    out_ref[...] = (a_ref[...].astype(F32) + b_ref[...].astype(F32)).astype(BF16)


def mask_kernel(plane_ref, ids_ref, probs_ref, pick_ref, weight_ref):
    step, place = arriving(iota(weight_ref.shape, 0))
    expert = block_index(step, place, plane_ref[0], weight_ref.shape[0]) * EXP_DEV
    pick, gate, first, _ = routing(ids_ref, probs_ref, expert)
    pick_ref[...] = zero_one(pick)
    weight_ref[...] = jnp.where(pick & first, gate, 0.0)


def combine_kernel(plane_ref, ids_ref, pick_ref, weight_ref, cot_ref, home_ref, mixed_ref, latgrad_ref, gate_ref):
    rows, wide = home_ref.shape
    weight = weight_ref[...]
    pick = pick_ref[...].astype(F32)
    row = iota(weight.shape, 0)
    step, place = arriving(row)
    expert = block_index(step, place, plane_ref[0], rows) * EXP_DEV
    first = (row & 2) == 0
    low = (row & 4) == 0
    home = home_ref[...]
    chosen = jnp.where(first, pick, 0.0)
    token = pick - chosen
    inner = jnp.zeros(weight.shape, F32)
    for h in range(2):
        here = low if h == 0 else ~low
        cols = pl.ds(h * wide, wide)
        high, rest = halves(jnp.where(here, weight, 0.0))
        mixed_ref[:, cols] = (mm(high, home, 0, 0) + mm(rest, home, 0, 0)).astype(BF16)
        latgrad_ref[:, cols] = mm(jnp.where(here, token, 0.0).astype(BF16), home, 0, 0).astype(BF16)
        inner = jnp.where(here, mm(home, cot_ref[:, cols], 1, 1), inner)
    inner = jnp.where(chosen > 0.5, inner, 0.0)
    for slot in range(ids_ref.shape[0]):
        hit = ids_ref[slot : slot + 1, :] == expert
        gate_ref[slot : slot + 1, :] = jnp.sum(jnp.where(hit, inner, 0.0), axis=0, keepdims=True)


def call(kernel, outs, scratch=(), specs=None, vmem=VMEM_BYTES):
    shapes = [jax.ShapeDtypeStruct(shape, dtype) for shape, dtype in outs]
    return pl.pallas_call(
        kernel,
        out_shape=shapes,
        in_specs=specs,
        out_specs=[pl.BlockSpec(memory_space=pltpu.VMEM)] * len(shapes),
        scratch_shapes=list(scratch),
        compiler_params=pltpu.CompilerParams(vmem_limit_bytes=vmem),
        name=kernel.__name__,
    )


def local(latent, expert_ids, gate_probs, cotangent, w_gate_up, w_down):
    tokens, lat = latent.shape
    top = expert_ids.shape[1]
    columns = lax.axis_size("expert")
    replicas = lax.axis_size("dp")
    ffw = w_down.shape[2]
    rows = columns * GROUP
    wide = lat // 2
    width = 3 * ffw
    share = lat // replicas
    ids = expert_ids.T
    probs = gate_probs.T
    vmem = pl.BlockSpec(memory_space=pltpu.VMEM)

    smem = pl.BlockSpec(memory_space=pltpu.SMEM)
    plane = (lax.axis_index("expert") // (columns // RING)).astype(jnp.int32).reshape(1)
    part = rows // RING
    leave = [((part, wide), BF16), ((part + part // 2, wide), BF16), ((part + part // 2, wide), BF16)]

    (sent,) = call(
        pack_kernel,
        [((rows, wide), BF16)],
        scratch=[pltpu.VMEM(a.shape, a.dtype) for a in (ids, probs, latent, cotangent)]
        + [pltpu.SemaphoreType.DMA((4,))],
        specs=[pl.BlockSpec(memory_space=pl.ANY)] * 4,
        vmem=ALL_VMEM_BYTES,
    )(ids, probs, latent, cotangent)
    there = lax.all_to_all(
        sent.reshape(columns, GROUP, wide), "expert", split_axis=0, concat_axis=0, tiled=True
    ).reshape(rows, wide)

    core = (lax.axis_index("dp") % 2).astype(jnp.int32).reshape(1)
    half_terms = ((replicas // 2, share, width), BF16)
    slots = columns * CAP
    mine, other, act, grad_hidden = call(
        expert_kernel,
        [half_terms, half_terms, ((slots, ffw), BF16), ((slots, 2 * ffw), BF16)],
        scratch=[pltpu.VMEM((lat, width), BF16)],
        vmem=ALL_VMEM_BYTES,
        specs=[smem] + [vmem] * 3,
    )(core, there, w_gate_up[0], w_down[0])

    swapped = lax.ppermute(other, "dp", [(i, i ^ 1) for i in range(replicas)])
    back = call(return_kernel, leave, specs=[smem] + [vmem] * 4, vmem=ALL_VMEM_BYTES)(
        plane, act, grad_hidden, w_gate_up[0], w_down[0]
    )
    (pair,) = call(add_kernel, [half_terms], specs=[vmem] * 2, vmem=ALL_VMEM_BYTES)(mine, swapped)
    pair, *back = lax.optimization_barrier((pair, *back))
    summed = lax.psum_scatter(
        pair.reshape(lat // 2, width), "dp", scatter_dimension=0, tiled=True,
        axis_index_groups=[list(range(c, replicas, 2)) for c in range(2)],
    )
    home = lax.cond(
        core[0] < 2,
        lambda stay, right, left: exchange(stay, right, left),
        lambda stay, right, left: jnp.concatenate([stay, right, left], axis=0),
        *back,
    )
    pick, weight = call(
        mask_kernel, [((rows, tokens), BF16), ((rows, tokens), F32)], specs=[smem] + [vmem] * 2
    )(plane, ids, probs)
    mixed, latent_gradient, gate_grad = call(
        combine_kernel,
        [((tokens, lat), BF16), ((tokens, lat), BF16), ((top, tokens), F32)],
        specs=[smem] + [vmem] * 5,
    )(plane, ids, pick, weight, cotangent, home)
    summed, mixed, latent_gradient, gate_grad = lax.optimization_barrier(
        (summed, mixed, latent_gradient, gate_grad)
    )
    gate_up_grad, down_grad = call(
        split_kernel,
        [((share, 2 * ffw), BF16), ((share, ffw), BF16)],
        scratch=[pltpu.SemaphoreType.DMA((2,))],
        specs=[pl.BlockSpec(memory_space=pl.ANY)],
        vmem=ALL_VMEM_BYTES,
    )(summed)
    return (mixed, latent_gradient, gate_grad.T, gate_up_grad[None], down_grad[None])


def exchange(stay, right, left):
    part, wide = stay.shape
    columns = lax.axis_size("expert")
    places = columns // RING
    up = [(e, (e + places) % columns) for e in range(columns)]
    down = [(e, (e - places) % columns) for e in range(columns)]
    half = part // 2
    one_right = lax.ppermute(right, "expert", up)
    one_left = lax.ppermute(left, "expert", down)
    two_right = lax.ppermute(one_right[part:], "expert", up)
    two_left = lax.ppermute(one_left[:half], "expert", down)
    pieces = [stay, one_right[:part], one_left[half:], jnp.concatenate([two_right, two_left], axis=0)]
    merged = jnp.concatenate([piece.reshape(places, GROUP, wide) for piece in pieces], axis=1)
    moved = lax.all_to_all(
        merged, "expert", split_axis=0, concat_axis=0, tiled=True,
        axis_index_groups=[list(range(z * places, (z + 1) * places)) for z in range(RING)],
    )
    return moved.reshape(RING * part, wide)


def solution(mesh):
    return jax.shard_map(
        local,
        mesh=mesh,
        in_specs=(
            P(("dp", "expert"), None),
            P(("dp", "expert"), None),
            P(("dp", "expert"), None),
            P(("dp", "expert"), None),
            P("expert", None, None),
            P("expert", None, None),
        ),
        out_specs=(
            P(("dp", "expert"), None),
            P(("dp", "expert"), None),
            P(("dp", "expert"), None),
            P("expert", "dp", None),
            P("expert", "dp", None),
        ),
        check_vma=False,
    )
```

```python
import jax
import jax.numpy as jnp
from jax import lax
from jax.experimental import pallas as pl
from jax.experimental.pallas import tpu as pltpu
from jax.sharding import PartitionSpec as P

EXP_DEV = 4
CAP = 2
GROUP = 4 * CAP
F32 = jnp.float32
BF16 = jnp.bfloat16
VMEM_BYTES = 48 << 20
ALL_VMEM_BYTES = 63 << 20


def mm(a, b, ca=1, cb=0):
    return lax.dot_general(a, b, (((ca,), (cb,)), ((), ())), preferred_element_type=F32)


def iota(shape, dim):
    return lax.broadcasted_iota(jnp.int32, shape, dim)


def halves(value):
    high = value.astype(BF16)
    return high, (value - high.astype(F32)).astype(BF16)


def routing(ids_ref, probs_ref, rows):
    tokens = ids_ref.shape[1]
    row = iota((rows, tokens), 0)
    expert = (row // GROUP) * EXP_DEV
    named = jnp.zeros((rows, tokens), F32)
    gate = jnp.zeros((rows, tokens), F32)
    for slot in range(ids_ref.shape[0]):
        hit = ids_ref[slot : slot + 1, :] == expert
        named = jnp.where(hit, 1.0, named)
        gate = jnp.where(hit, probs_ref[slot : slot + 1, :], gate)
    before = iota((tokens, tokens), 0)
    after = iota((tokens, tokens), 1)
    earlier = mm(named.astype(BF16), jnp.where(before < after, 1.0, 0.0).astype(BF16))
    pick = (named > 0.5) & (earlier == (row & 1).astype(F32))
    kind = (row & 2) == 0
    half = (row & 4) == 0
    return pick, gate, kind, half, expert


def zero_one(mask):
    return jnp.where(mask, 1.0, 0.0).astype(BF16)


def pack_kernel(ids_hbm, probs_hbm, latent_hbm, cot_hbm, sent_ref, ids_ref, probs_ref, latent_ref, cot_ref, sems):
    rows, wide = sent_ref.shape
    pairs = [(ids_hbm, ids_ref), (probs_hbm, probs_ref), (latent_hbm, latent_ref), (cot_hbm, cot_ref)]
    copies = [pltpu.make_async_copy(a, b, sems.at[i]) for i, (a, b) in enumerate(pairs)]
    for copy in copies:
        copy.start()
    copies[0].wait()
    copies[1].wait()
    pick, gate, first, low, _ = routing(ids_ref, probs_ref, rows)
    token = jnp.where(pick & first, 1.0, 0.0)
    weight = jnp.where(pick & ~first, gate, 0.0)
    copies[2].wait()
    copies[3].wait()
    total = jnp.zeros((rows, wide), F32)
    for h in range(2):
        here = low if h == 0 else ~low
        high, rest = halves(jnp.where(here, weight, 0.0))
        picks = jnp.concatenate([jnp.where(here, token, 0.0).astype(BF16), high, rest], axis=1)
        cols = pl.ds(h * wide, wide)
        cot = cot_ref[:, cols]
        total = total + mm(picks, jnp.concatenate([latent_ref[:, cols], cot, cot], axis=0))
    sent_ref[...] = total.astype(BF16)


def sorted_position(index, slots):
    group = index // GROUP
    return ((index & 2) + ((index >> 2) & 1)) * slots + group * CAP + (index & 1)


def line_ring(chips):
    return list(range(0, chips, 2)) + list(range(1, chips, 2))[::-1]


def expert_kernel(
    core_ref, there_ref, win_ref, wout_ref, mine_ref, other_ref, act_ref, grad_ref, terms_ref
):
    rows, wide = there_ref.shape
    slots = rows // 4
    ffw = wout_ref.shape[1]
    share = mine_ref.shape[1]
    sort = zero_one(iota((rows, rows), 0) == sorted_position(iota((rows, rows), 1), slots))
    data = mm(sort, there_ref[...]).astype(BF16)
    vec = [data[:slots], data[slots : 2 * slots]]
    cot = [data[2 * slots : 3 * slots], data[3 * slots :]]
    top = [pl.ds(0, wide), pl.ds(wide, wide)]

    hidden = mm(vec[0], win_ref[top[0], :]) + mm(vec[1], win_ref[top[1], :])
    g = hidden[:, :ffw]
    u = hidden[:, ffw:]
    s = 1.0 / (1.0 + jnp.exp(-g))
    act = (g * s * u).astype(BF16)
    grad_act = mm(cot[0], wout_ref[top[0], :]) + mm(cot[1], wout_ref[top[1], :])
    grad_hidden = jnp.concatenate(
        [grad_act * u * s * (1.0 + g * (1.0 - s)), grad_act * g * s], axis=1
    ).astype(BF16)
    act_ref[...] = act
    grad_ref[...] = grad_hidden

    for h in range(2):
        terms_ref[top[h], : 2 * ffw] = mm(vec[h], grad_hidden, 0, 0).astype(BF16)
        terms_ref[top[h], 2 * ffw :] = mm(cot[h], act, 0, 0).astype(BF16)
    even = core_ref[0] == 0
    for block, chip in enumerate(line_ring(mine_ref.shape[0])):
        a = terms_ref[pl.ds(2 * chip * share, share), :]
        b = terms_ref[pl.ds((2 * chip + 1) * share, share), :]
        mine_ref[block] = jnp.where(even, a, b)
        other_ref[block] = jnp.where(even, b, a)


def return_kernel(act_ref, grad_ref, win_ref, wout_ref, back_ref):
    rows, wide = back_ref.shape
    slots = rows // 4
    top = [pl.ds(0, wide), pl.ds(wide, wide)]
    act = act_ref[...]
    grad_hidden = grad_ref[...]
    result = jnp.concatenate(
        [mm(act, wout_ref[top[h], :], 1, 1).astype(BF16) for h in range(2)]
        + [mm(grad_hidden, win_ref[top[h], :], 1, 1).astype(BF16) for h in range(2)],
        axis=0,
    )
    unsort = zero_one(iota((rows, rows), 1) == sorted_position(iota((rows, rows), 0), slots))
    back_ref[...] = mm(unsort, result).astype(BF16)


def split_kernel(sum_hbm, gate_up_ref, down_ref, sems):
    cut = gate_up_ref.shape[1]
    copies = [
        pltpu.make_async_copy(sum_hbm.at[:, pl.ds(0, cut)], gate_up_ref, sems.at[0]),
        pltpu.make_async_copy(sum_hbm.at[:, pl.ds(cut, down_ref.shape[1])], down_ref, sems.at[1]),
    ]
    for copy in copies:
        copy.start()
    for copy in copies:
        copy.wait()


def add_kernel(a_ref, b_ref, out_ref):
    out_ref[...] = (a_ref[...].astype(F32) + b_ref[...].astype(F32)).astype(BF16)


def mask_kernel(ids_ref, probs_ref, pick_ref, weight_ref):
    pick, gate, first, _, _ = routing(ids_ref, probs_ref, weight_ref.shape[0])
    pick_ref[...] = zero_one(pick)
    weight_ref[...] = jnp.where(pick & first, gate, 0.0)


def combine_kernel(ids_ref, pick_ref, weight_ref, cot_ref, home_ref, mixed_ref, latgrad_ref, gate_ref):
    rows, wide = home_ref.shape
    weight = weight_ref[...]
    pick = pick_ref[...].astype(F32)
    row = iota(weight.shape, 0)
    expert = (row // GROUP) * EXP_DEV
    first = (row & 2) == 0
    low = (row & 4) == 0
    home = home_ref[...]
    chosen = jnp.where(first, pick, 0.0)
    token = pick - chosen
    inner = jnp.zeros(weight.shape, F32)
    for h in range(2):
        here = low if h == 0 else ~low
        cols = pl.ds(h * wide, wide)
        high, rest = halves(jnp.where(here, weight, 0.0))
        mixed_ref[:, cols] = (mm(high, home, 0, 0) + mm(rest, home, 0, 0)).astype(BF16)
        latgrad_ref[:, cols] = mm(jnp.where(here, token, 0.0).astype(BF16), home, 0, 0).astype(BF16)
        inner = jnp.where(here, mm(home, cot_ref[:, cols], 1, 1), inner)
    inner = jnp.where(chosen > 0.5, inner, 0.0)
    for slot in range(ids_ref.shape[0]):
        hit = ids_ref[slot : slot + 1, :] == expert
        gate_ref[slot : slot + 1, :] = jnp.sum(jnp.where(hit, inner, 0.0), axis=0, keepdims=True)


def call(kernel, outs, scratch=(), specs=None, vmem=VMEM_BYTES):
    shapes = [jax.ShapeDtypeStruct(shape, dtype) for shape, dtype in outs]
    return pl.pallas_call(
        kernel,
        out_shape=shapes,
        in_specs=specs,
        out_specs=[pl.BlockSpec(memory_space=pltpu.VMEM)] * len(shapes),
        scratch_shapes=list(scratch),
        compiler_params=pltpu.CompilerParams(vmem_limit_bytes=vmem),
        name=kernel.__name__,
    )


def local(latent, expert_ids, gate_probs, cotangent, w_gate_up, w_down):
    tokens, lat = latent.shape
    top = expert_ids.shape[1]
    columns = lax.axis_size("expert")
    replicas = lax.axis_size("dp")
    ffw = w_down.shape[2]
    rows = columns * GROUP
    wide = lat // 2
    width = 3 * ffw
    share = lat // replicas
    ids = expert_ids.T
    probs = gate_probs.T
    vmem = pl.BlockSpec(memory_space=pltpu.VMEM)

    (sent,) = call(
        pack_kernel,
        [((rows, wide), BF16)],
        scratch=[pltpu.VMEM(a.shape, a.dtype) for a in (ids, probs, latent, cotangent)]
        + [pltpu.SemaphoreType.DMA((4,))],
        specs=[pl.BlockSpec(memory_space=pl.ANY)] * 4,
        vmem=ALL_VMEM_BYTES,
    )(ids, probs, latent, cotangent)
    there = exchange(sent, columns)

    core = (lax.axis_index("dp") % 2).astype(jnp.int32).reshape(1)
    half_terms = ((replicas // 2, share, width), BF16)
    slots = columns * CAP
    mine, other, act, grad_hidden = call(
        expert_kernel,
        [half_terms, half_terms, ((slots, ffw), BF16), ((slots, 2 * ffw), BF16)],
        scratch=[pltpu.VMEM((lat, width), BF16)],
        specs=[pl.BlockSpec(memory_space=pltpu.SMEM)] + [vmem] * 3,
    )(core, there, w_gate_up[0], w_down[0])

    swapped = lax.ppermute(other, "dp", [(i, i ^ 1) for i in range(replicas)])
    (back,) = call(return_kernel, [((rows, wide), BF16)], specs=[vmem] * 4)(
        act, grad_hidden, w_gate_up[0], w_down[0]
    )
    (pair,) = call(add_kernel, [half_terms], specs=[vmem] * 2)(mine, swapped)
    pair, back = lax.optimization_barrier((pair, back))
    summed = lax.psum_scatter(
        pair.reshape(lat // 2, width), "dp", scatter_dimension=0, tiled=True,
        axis_index_groups=[[2 * chip + c for chip in line_ring(replicas // 2)] for c in range(2)],
    )
    home = lax.cond(core[0] < 2, lambda b: exchange(b, columns), lambda b: b, back)
    pick, weight = call(
        mask_kernel, [((rows, tokens), BF16), ((rows, tokens), F32)], specs=[vmem] * 2
    )(ids, probs)
    mixed, latent_gradient, gate_grad = call(
        combine_kernel,
        [((tokens, lat), BF16), ((tokens, lat), BF16), ((top, tokens), F32)],
        specs=[vmem] * 5,
    )(ids, pick, weight, cotangent, home)
    summed, mixed, latent_gradient, gate_grad = lax.optimization_barrier(
        (summed, mixed, latent_gradient, gate_grad)
    )
    gate_up_grad, down_grad = call(
        split_kernel,
        [((share, 2 * ffw), BF16), ((share, ffw), BF16)],
        scratch=[pltpu.SemaphoreType.DMA((2,))],
        specs=[pl.BlockSpec(memory_space=pl.ANY)],
        vmem=ALL_VMEM_BYTES,
    )(summed)
    return (mixed, latent_gradient, gate_grad.T, gate_up_grad[None], down_grad[None])


def exchange(message, columns):
    rows, wide = message.shape
    moved = lax.all_to_all(
        message.reshape(columns, rows // columns, wide), "expert", split_axis=0, concat_axis=0, tiled=True
    )
    return moved.reshape(rows, wide)


def solution(mesh):
    return jax.shard_map(
        local,
        mesh=mesh,
        in_specs=(
            P(("dp", "expert"), None),
            P(("dp", "expert"), None),
            P(("dp", "expert"), None),
            P(("dp", "expert"), None),
            P("expert", None, None),
            P("expert", None, None),
        ),
        out_specs=(
            P(("dp", "expert"), None),
            P(("dp", "expert"), None),
            P(("dp", "expert"), None),
            P("expert", "dp", None),
            P("expert", "dp", None),
        ),
        check_vma=False,
    )
```

```python
import jax
import jax.numpy as jnp
from jax import lax
from jax.experimental import pallas as pl
from jax.experimental.pallas import tpu as pltpu
from jax.sharding import PartitionSpec as P

EXP_DEV = 4
CAP = 2
GROUP = 4 * CAP
RING = 4
F32 = jnp.float32
BF16 = jnp.bfloat16
VMEM_BYTES = 48 << 20
ALL_VMEM_BYTES = 63 << 20


def mm(a, b, ca=1, cb=0):
    return lax.dot_general(a, b, (((ca,), (cb,)), ((), ())), preferred_element_type=F32)


def iota(shape, dim):
    return lax.broadcasted_iota(jnp.int32, shape, dim)


def halves(value):
    high = value.astype(BF16)
    return high, (value - high.astype(F32)).astype(BF16)


def leaving(row, rows):
    part = rows // RING
    return row // part, (row % part) // GROUP


def arriving(row):
    piece = (row // GROUP) % RING
    step = jnp.where(piece == 0, 0, jnp.where(piece == 1, RING - 1, piece - 1))
    return step, row // (GROUP * RING)


def block_index(step, place, plane, rows):
    return ((plane + step) % RING) * (rows // (GROUP * RING)) + place


def routing(ids_ref, probs_ref, expert):
    rows, tokens = expert.shape
    row = iota((rows, tokens), 0)
    named = jnp.zeros((rows, tokens), F32)
    gate = jnp.zeros((rows, tokens), F32)
    for slot in range(ids_ref.shape[0]):
        hit = ids_ref[slot : slot + 1, :] == expert
        named = jnp.where(hit, 1.0, named)
        gate = jnp.where(hit, probs_ref[slot : slot + 1, :], gate)
    before = iota((tokens, tokens), 0)
    after = iota((tokens, tokens), 1)
    earlier = mm(named.astype(BF16), jnp.where(before < after, 1.0, 0.0).astype(BF16))
    pick = (named > 0.5) & (earlier == (row & 1).astype(F32))
    kind = (row & 2) == 0
    half = (row & 4) == 0
    return pick, gate, kind, half


def zero_one(mask):
    return jnp.where(mask, 1.0, 0.0).astype(BF16)


def store_leaving(message, stay_ref, right_ref, left_ref):
    part = stay_ref.shape[0]
    middle = 2 * part + part // 2
    stay_ref[...] = message[:part]
    right_ref[...] = message[part:middle]
    left_ref[...] = message[middle:]


def pack_kernel(ids_hbm, probs_hbm, latent_hbm, cot_hbm, sent_ref, ids_ref, probs_ref, latent_ref, cot_ref, sems):
    rows, wide = sent_ref.shape
    pairs = [(ids_hbm, ids_ref), (probs_hbm, probs_ref), (latent_hbm, latent_ref), (cot_hbm, cot_ref)]
    copies = [pltpu.make_async_copy(a, b, sems.at[i]) for i, (a, b) in enumerate(pairs)]
    for copy in copies:
        copy.start()
    copies[0].wait()
    copies[1].wait()
    expert = iota((rows, ids_ref.shape[1]), 0) // GROUP * EXP_DEV
    pick, gate, first, low = routing(ids_ref, probs_ref, expert)
    token = jnp.where(pick & first, 1.0, 0.0)
    weight = jnp.where(pick & ~first, gate, 0.0)
    copies[2].wait()
    copies[3].wait()
    total = jnp.zeros((rows, wide), F32)
    for h in range(2):
        here = low if h == 0 else ~low
        high, rest = halves(jnp.where(here, weight, 0.0))
        picks = jnp.concatenate([jnp.where(here, token, 0.0).astype(BF16), high, rest], axis=1)
        cols = pl.ds(h * wide, wide)
        cot = cot_ref[:, cols]
        total = total + mm(picks, jnp.concatenate([latent_ref[:, cols], cot, cot], axis=0))
    sent_ref[...] = total.astype(BF16)


def sorted_position(index, slots):
    group = index // GROUP
    return ((index & 2) + ((index >> 2) & 1)) * slots + group * CAP + (index & 1)


def line_ring(chips):
    return list(range(0, chips, 2)) + list(range(1, chips, 2))[::-1]


def expert_kernel(
    core_ref, there_ref, win_ref, wout_ref, mine_ref, other_ref, act_ref, grad_ref, terms_ref
):
    rows, wide = there_ref.shape
    slots = rows // 4
    ffw = wout_ref.shape[1]
    share = mine_ref.shape[1]
    sort = zero_one(iota((rows, rows), 0) == sorted_position(iota((rows, rows), 1), slots))
    data = mm(sort, there_ref[...]).astype(BF16)
    vec = [data[:slots], data[slots : 2 * slots]]
    cot = [data[2 * slots : 3 * slots], data[3 * slots :]]
    top = [pl.ds(0, wide), pl.ds(wide, wide)]

    hidden = mm(vec[0], win_ref[top[0], :]) + mm(vec[1], win_ref[top[1], :])
    g = hidden[:, :ffw]
    u = hidden[:, ffw:]
    s = 1.0 / (1.0 + jnp.exp(-g))
    act = (g * s * u).astype(BF16)
    grad_act = mm(cot[0], wout_ref[top[0], :]) + mm(cot[1], wout_ref[top[1], :])
    grad_hidden = jnp.concatenate(
        [grad_act * u * s * (1.0 + g * (1.0 - s)), grad_act * g * s], axis=1
    ).astype(BF16)
    act_ref[...] = act
    grad_ref[...] = grad_hidden

    for h in range(2):
        terms_ref[top[h], : 2 * ffw] = mm(vec[h], grad_hidden, 0, 0).astype(BF16)
        terms_ref[top[h], 2 * ffw :] = mm(cot[h], act, 0, 0).astype(BF16)
    even = core_ref[0] == 0
    for block, chip in enumerate(line_ring(mine_ref.shape[0])):
        a = terms_ref[pl.ds(2 * chip * share, share), :]
        b = terms_ref[pl.ds((2 * chip + 1) * share, share), :]
        mine_ref[block] = jnp.where(even, a, b)
        other_ref[block] = jnp.where(even, b, a)


def return_kernel(plane_ref, act_ref, grad_ref, win_ref, wout_ref, stay_ref, right_ref, left_ref):
    part, wide = stay_ref.shape
    rows = RING * part
    slots = rows // 4
    top = [pl.ds(0, wide), pl.ds(wide, wide)]
    act = act_ref[...]
    grad_hidden = grad_ref[...]
    result = jnp.concatenate(
        [mm(act, wout_ref[top[h], :], 1, 1).astype(BF16) for h in range(2)]
        + [mm(grad_hidden, win_ref[top[h], :], 1, 1).astype(BF16) for h in range(2)],
        axis=0,
    )
    row = iota((rows, rows), 0)
    step, place = leaving(row, rows)
    source = block_index(step, place, plane_ref[0], rows) * GROUP + row % GROUP
    unsort = zero_one(iota((rows, rows), 1) == sorted_position(source, slots))
    store_leaving(mm(unsort, result).astype(BF16), stay_ref, right_ref, left_ref)


def split_kernel(sum_hbm, gate_up_ref, down_ref, sems):
    cut = gate_up_ref.shape[1]
    copies = [
        pltpu.make_async_copy(sum_hbm.at[:, pl.ds(0, cut)], gate_up_ref, sems.at[0]),
        pltpu.make_async_copy(sum_hbm.at[:, pl.ds(cut, down_ref.shape[1])], down_ref, sems.at[1]),
    ]
    for copy in copies:
        copy.start()
    for copy in copies:
        copy.wait()


def add_kernel(a_ref, b_ref, out_ref):
    out_ref[...] = (a_ref[...].astype(F32) + b_ref[...].astype(F32)).astype(BF16)


def mask_kernel(plane_ref, ids_ref, probs_ref, pick_ref, weight_ref):
    step, place = arriving(iota(weight_ref.shape, 0))
    expert = block_index(step, place, plane_ref[0], weight_ref.shape[0]) * EXP_DEV
    pick, gate, first, _ = routing(ids_ref, probs_ref, expert)
    pick_ref[...] = zero_one(pick)
    weight_ref[...] = jnp.where(pick & first, gate, 0.0)


def combine_kernel(plane_ref, ids_ref, pick_ref, weight_ref, cot_ref, home_ref, mixed_ref, latgrad_ref, gate_ref):
    rows, wide = home_ref.shape
    weight = weight_ref[...]
    pick = pick_ref[...].astype(F32)
    row = iota(weight.shape, 0)
    step, place = arriving(row)
    expert = block_index(step, place, plane_ref[0], rows) * EXP_DEV
    first = (row & 2) == 0
    low = (row & 4) == 0
    home = home_ref[...]
    chosen = jnp.where(first, pick, 0.0)
    token = pick - chosen
    inner = jnp.zeros(weight.shape, F32)
    for h in range(2):
        here = low if h == 0 else ~low
        cols = pl.ds(h * wide, wide)
        high, rest = halves(jnp.where(here, weight, 0.0))
        mixed_ref[:, cols] = (mm(high, home, 0, 0) + mm(rest, home, 0, 0)).astype(BF16)
        latgrad_ref[:, cols] = mm(jnp.where(here, token, 0.0).astype(BF16), home, 0, 0).astype(BF16)
        inner = jnp.where(here, mm(home, cot_ref[:, cols], 1, 1), inner)
    inner = jnp.where(chosen > 0.5, inner, 0.0)
    for slot in range(ids_ref.shape[0]):
        hit = ids_ref[slot : slot + 1, :] == expert
        gate_ref[slot : slot + 1, :] = jnp.sum(jnp.where(hit, inner, 0.0), axis=0, keepdims=True)


def call(kernel, outs, scratch=(), specs=None, vmem=VMEM_BYTES):
    shapes = [jax.ShapeDtypeStruct(shape, dtype) for shape, dtype in outs]
    return pl.pallas_call(
        kernel,
        out_shape=shapes,
        in_specs=specs,
        out_specs=[pl.BlockSpec(memory_space=pltpu.VMEM)] * len(shapes),
        scratch_shapes=list(scratch),
        compiler_params=pltpu.CompilerParams(vmem_limit_bytes=vmem),
        name=kernel.__name__,
    )


def local(latent, expert_ids, gate_probs, cotangent, w_gate_up, w_down):
    tokens, lat = latent.shape
    top = expert_ids.shape[1]
    columns = lax.axis_size("expert")
    replicas = lax.axis_size("dp")
    ffw = w_down.shape[2]
    rows = columns * GROUP
    wide = lat // 2
    width = 3 * ffw
    share = lat // replicas
    ids = expert_ids.T
    probs = gate_probs.T
    vmem = pl.BlockSpec(memory_space=pltpu.VMEM)

    smem = pl.BlockSpec(memory_space=pltpu.SMEM)
    plane = (lax.axis_index("expert") // (columns // RING)).astype(jnp.int32).reshape(1)
    part = rows // RING
    leave = [((part, wide), BF16), ((part + part // 2, wide), BF16), ((part + part // 2, wide), BF16)]

    (sent,) = call(
        pack_kernel,
        [((rows, wide), BF16)],
        scratch=[pltpu.VMEM(a.shape, a.dtype) for a in (ids, probs, latent, cotangent)]
        + [pltpu.SemaphoreType.DMA((4,))],
        specs=[pl.BlockSpec(memory_space=pl.ANY)] * 4,
        vmem=ALL_VMEM_BYTES,
    )(ids, probs, latent, cotangent)
    there = lax.all_to_all(
        sent.reshape(columns, GROUP, wide), "expert", split_axis=0, concat_axis=0, tiled=True
    ).reshape(rows, wide)

    core = (lax.axis_index("dp") % 2).astype(jnp.int32).reshape(1)
    half_terms = ((replicas // 2, share, width), BF16)
    slots = columns * CAP
    mine, other, act, grad_hidden = call(
        expert_kernel,
        [half_terms, half_terms, ((slots, ffw), BF16), ((slots, 2 * ffw), BF16)],
        scratch=[pltpu.VMEM((lat, width), BF16)],
        vmem=ALL_VMEM_BYTES,
        specs=[smem] + [vmem] * 3,
    )(core, there, w_gate_up[0], w_down[0])

    swapped = lax.ppermute(other, "dp", [(i, i ^ 1) for i in range(replicas)])
    back = call(return_kernel, leave, specs=[smem] + [vmem] * 4, vmem=ALL_VMEM_BYTES)(
        plane, act, grad_hidden, w_gate_up[0], w_down[0]
    )
    (pair,) = call(add_kernel, [half_terms], specs=[vmem] * 2, vmem=ALL_VMEM_BYTES)(mine, swapped)
    pair, *back = lax.optimization_barrier((pair, *back))
    summed = lax.psum_scatter(
        pair.reshape(lat // 2, width), "dp", scatter_dimension=0, tiled=True,
        axis_index_groups=[[2 * chip + c for chip in line_ring(replicas // 2)] for c in range(2)],
    )
    home = lax.cond(
        core[0] < 2,
        lambda stay, right, left: exchange(stay, right, left),
        lambda stay, right, left: jnp.concatenate([stay, right, left], axis=0),
        *back,
    )
    pick, weight = call(
        mask_kernel, [((rows, tokens), BF16), ((rows, tokens), F32)], specs=[smem] + [vmem] * 2
    )(plane, ids, probs)
    mixed, latent_gradient, gate_grad = call(
        combine_kernel,
        [((tokens, lat), BF16), ((tokens, lat), BF16), ((top, tokens), F32)],
        specs=[smem] + [vmem] * 5,
    )(plane, ids, pick, weight, cotangent, home)
    summed, mixed, latent_gradient, gate_grad = lax.optimization_barrier(
        (summed, mixed, latent_gradient, gate_grad)
    )
    gate_up_grad, down_grad = call(
        split_kernel,
        [((share, 2 * ffw), BF16), ((share, ffw), BF16)],
        scratch=[pltpu.SemaphoreType.DMA((2,))],
        specs=[pl.BlockSpec(memory_space=pl.ANY)],
        vmem=ALL_VMEM_BYTES,
    )(summed)
    return (mixed, latent_gradient, gate_grad.T, gate_up_grad[None], down_grad[None])


def exchange(stay, right, left):
    part, wide = stay.shape
    columns = lax.axis_size("expert")
    places = columns // RING
    up = [(e, (e + places) % columns) for e in range(columns)]
    down = [(e, (e - places) % columns) for e in range(columns)]
    half = part // 2
    one_right = lax.ppermute(right, "expert", up)
    one_left = lax.ppermute(left, "expert", down)
    two_right = lax.ppermute(one_right[part:], "expert", up)
    two_left = lax.ppermute(one_left[:half], "expert", down)
    pieces = [stay, one_right[:part], one_left[half:], jnp.concatenate([two_right, two_left], axis=0)]
    merged = jnp.concatenate([piece.reshape(places, GROUP, wide) for piece in pieces], axis=1)
    moved = lax.all_to_all(
        merged, "expert", split_axis=0, concat_axis=0, tiled=True,
        axis_index_groups=[list(range(z * places, (z + 1) * places)) for z in range(RING)],
    )
    return moved.reshape(RING * part, wide)


def solution(mesh):
    return jax.shard_map(
        local,
        mesh=mesh,
        in_specs=(
            P(("dp", "expert"), None),
            P(("dp", "expert"), None),
            P(("dp", "expert"), None),
            P(("dp", "expert"), None),
            P("expert", None, None),
            P("expert", None, None),
        ),
        out_specs=(
            P(("dp", "expert"), None),
            P(("dp", "expert"), None),
            P(("dp", "expert"), None),
            P("expert", "dp", None),
            P("expert", "dp", None),
        ),
        check_vma=False,
    )
```
